32 devices in a mesh: band: 2 (over x), gx: 16 (over z, y, core).
Axes of the slice: x: 2, y: 2, z: 4, core: 2. Of those that a mesh axis runs over, the one named last changes fastest.
Arguments:
- slc_tiles: bfloat16 [64, 2, 64, 2048], P('gx', None, 'band'), parts along dimension 2, may hold values from -64 to 64
- look_weight: float32 [64, 2048], P('band'), parts along dimension 0, may hold values from 0.05 to 1
- pair_list: int32 [192, 2], replicated, may hold values from 0 to 63, as said below
Outputs:
- corrected: float32 [64, 64, 2048], P(None, 'band', 'gx'), parts along dimension 1
The draws below stay inside these ranges and needn't reach their ends.
There are 2 independent parts, one for each index of `band`. The reference program is written for one: setup_inputs(seed, part) draws one part's arguments, and reference() takes and returns one part's arrays. A program takes and returns all parts, laid end to end along the dimension named above; an argument that names none is the same for every part. Nothing has to cross between parts.
Inputs may be any that keep to these rules, and one draw needn't show every extreme that they name: `pair_list`: row p is a pair of date indices; with d = p // 12, the reference date lies in d * 4 to (d + 1) * 4 - 1 and the secondary date is 1 to 4 dates after it.
All inputs are finite; a program needn't handle non-finite values.
Results may differ from the reference program's by a relative error of at most 0.0071.
Values may be sent and summed in bfloat16 or wider, within the bound.
A program may use at most 128 MiB of HBM per device.

```python
import math
import jax
import jax.numpy as jnp
from jax import lax

DATE_DEV = 4
ROWS = 32
LOOK = 9
DATES = 64
PAIR_DEV = 12
PAIRS = 192
COLS = 2048


def draw_slc_tiles(key, part):
    subkeys = jax.random.split(key, 10)
    col_coord = (2.0 * jnp.arange(COLS, dtype=jnp.float32) + 1.0) / COLS - 1.0
    date_index = jnp.arange(DATES, dtype=jnp.float32)[:, None, None]
    scatter_re = jax.random.normal(subkeys[0], (ROWS, COLS), jnp.float32)
    scatter_im = jax.random.normal(subkeys[1], (ROWS, COLS), jnp.float32)
    amplitude = jnp.exp(jax.random.uniform(subkeys[2], (ROWS, COLS), jnp.float32, -1.2, 1.2))
    noise_re = 0.4 * jax.random.normal(subkeys[8], (DATES, ROWS, COLS), jnp.float32)
    noise_im = 0.4 * jax.random.normal(subkeys[9], (DATES, ROWS, COLS), jnp.float32)
    offsets = jax.random.uniform(subkeys[3], (DATES, 1, 1), jnp.float32, -1.0, 1.0)
    slopes = jax.random.uniform(subkeys[4], (DATES, 1, 1), jnp.float32, -1.5, 1.5)
    motion = jax.random.uniform(subkeys[5], (ROWS, COLS), jnp.float32, -1.0, 1.0) * (2.0 / DATES)
    rough = 0.4 * jax.random.normal(subkeys[6], (DATES, ROWS, COLS), jnp.float32)
    phase = offsets + slopes * col_coord + motion * date_index + rough
    cosine = jnp.cos(phase)
    sine = jnp.sin(phase)
    real_part = amplitude * (scatter_re * cosine - scatter_im * sine) + noise_re
    imag_part = amplitude * (scatter_re * sine + scatter_im * cosine) + noise_im
    stacked = jnp.clip(jnp.stack([real_part, imag_part], axis=1), -64.0, 64.0)
    return stacked.astype(jnp.bfloat16)


def draw_pair_list(key, part):
    subkeys = jax.random.split(key, 2)
    row_index = jnp.arange(PAIRS, dtype=jnp.int32)
    first_date = row_index // PAIR_DEV * DATE_DEV
    local_offset = jax.random.randint(subkeys[0], (PAIRS,), 0, DATE_DEV, dtype=jnp.int32)
    local_offset = jnp.where(row_index % PAIR_DEV == 0, 0, local_offset)
    reference_date = jnp.minimum(first_date + local_offset, DATES - 2)
    date_lag = jax.random.randint(subkeys[1], (PAIRS,), 1, DATE_DEV + 1, dtype=jnp.int32)
    secondary = jnp.minimum(reference_date + date_lag, DATES - 1)
    return jnp.stack([reference_date, secondary], axis=1).astype(jnp.int32)


def setup_inputs(seed: int = 0, part: int = 0) -> dict:
    arg_keys = jax.random.split(jax.random.key(seed), 4)
    part_splits = jax.random.split(jax.random.fold_in(arg_keys[3], part), 4)
    slc_tiles = draw_slc_tiles(jax.random.fold_in(jax.random.fold_in(arg_keys[3], part), 71), part)
    look_weight = jnp.clip(jnp.exp(jax.random.uniform(part_splits[1], (ROWS, COLS), jnp.float32, math.log(0.05), math.log(1.0))), 0.05, 1.0)
    pair_list = draw_pair_list(jax.random.fold_in(arg_keys[3], 71), part)
    return dict(slc_tiles=slc_tiles, look_weight=look_weight, pair_list=pair_list)


def box_sum(values, col_count):
    rim_width = LOOK // 2
    row_count = values.shape[-2]
    padded = jnp.pad(values, [(0, 0)] * (values.ndim - 2) + [(rim_width, rim_width), (0, 0)])
    running = padded[..., 0:row_count, :]
    for offset in range(1, LOOK):
        running = running + padded[..., offset:offset + row_count, :]
    summed = running[..., 0:col_count]
    for offset in range(1, LOOK):
        summed = summed + running[..., offset:offset + col_count]
    return summed

def observe(first_tile, second_tile, weight, col_count):
    first_re = first_tile[..., 0, :, :].astype(jnp.float32)
    first_im = first_tile[..., 1, :, :].astype(jnp.float32)
    second_re = second_tile[..., 0, :, :].astype(jnp.float32)
    second_im = second_tile[..., 1, :, :].astype(jnp.float32)
    cross_re = weight * (first_re * second_re + first_im * second_im)
    cross_im = weight * (first_im * second_re - first_re * second_im)
    power_first = weight * (first_re * first_re + first_im * first_im)
    power_second = weight * (second_re * second_re + second_im * second_im)
    stacked = jnp.stack([cross_re, cross_im, power_first, power_second], axis=0)
    looked = box_sum(stacked, col_count)
    return (looked[1] * lax.rsqrt(looked[2] * looked[3] + 1e-06)).astype(jnp.bfloat16)

def solve_normal(normal_matrix, projected):
    factor = jnp.linalg.cholesky(normal_matrix)
    return jax.scipy.linalg.cho_solve((factor, True), projected)

def reference(slc_tiles, look_weight, pair_list):
    rim_width = LOOK // 2
    tiles_pad = jnp.pad(slc_tiles, ((0, 0), (0, 0), (0, 0), (rim_width, rim_width)))
    weight_pad = jnp.pad(look_weight, ((0, 0), (rim_width, rim_width)))

    def one_pair(pair_row):
        return observe(tiles_pad[pair_row[0]], tiles_pad[pair_row[1]], weight_pad, COLS)
    observed = lax.map(one_pair, pair_list)
    date_ids = jnp.arange(DATES, dtype=jnp.int32)
    incidence = ((date_ids[:, None] == pair_list[None, :, 0]).astype(jnp.float32) - (date_ids[:, None] == pair_list[None, :, 1]).astype(jnp.float32)).astype(jnp.bfloat16)
    normal_matrix = jnp.dot(incidence.astype(jnp.float32), incidence.T.astype(jnp.float32), preferred_element_type=jnp.float32) + jnp.eye(DATES, dtype=jnp.float32)
    projected = jnp.dot(incidence.astype(jnp.float32), observed.reshape(PAIRS, ROWS * COLS).astype(jnp.float32), preferred_element_type=jnp.float32)
    series = solve_normal(normal_matrix, projected).reshape(DATES, ROWS, COLS)
    columns = (2.0 * jnp.arange(COLS, dtype=jnp.int32).astype(jnp.float32) + 1.0) / COLS - 1.0
    square_sum = jnp.sum(columns * columns)
    date_mean = lax.optimization_barrier(jnp.sum(series, axis=(1, 2))) / (ROWS * COLS)
    date_slope = lax.optimization_barrier(jnp.sum(series * columns, axis=(1, 2))) / (ROWS * square_sum)
    return series - date_mean[:, None, None] - date_slope[:, None, None] * columns
```

```python
import functools
import math

import jax
import jax.numpy as jnp
from jax import lax
from jax.experimental import pallas as pl
from jax.experimental.pallas import tpu as pltpu
from jax.sharding import PartitionSpec as P

LOOK = 9
RIM = LOOK // 2
LAGS = 4
MESH = pl.DeviceIdType.MESH
F32 = jnp.float32
BF16 = jnp.bfloat16
HIGHEST = lax.Precision.HIGHEST
MIB = 1024 * 1024


def greet_all(n, band, me):
    barrier = pltpu.get_barrier_semaphore()

    def greet(k, carry):
        peer = lax.rem(me + k, n)
        pl.semaphore_signal(barrier, inc=1, device_id=(band, peer), device_id_type=MESH)
        return carry

    lax.fori_loop(1, n, greet, 0)
    pl.semaphore_wait(barrier, n - 1)


def network_weights(pairs, dates, degree_bound):
    pair_total = pairs.shape[0]
    first = pairs[:, 0:1]
    second = pairs[:, 1:2]
    ids = lax.broadcasted_iota(jnp.int32, (pair_total, dates), 1)
    incidence_t = (ids == first).astype(F32) - (ids == second).astype(F32)
    incidence = incidence_t.T
    product = jnp.dot(incidence.astype(BF16), incidence_t.astype(BF16), preferred_element_type=F32)
    row = lax.broadcasted_iota(jnp.int32, (dates, dates), 0)
    col = lax.broadcasted_iota(jnp.int32, (dates, dates), 1)
    eye = (row == col).astype(F32)
    normal = product + eye
    top = 1.0 + 2.0 * degree_bound
    scale = 2.0 / (1.0 + top)
    power = eye - normal * scale
    inverse = (eye + power) * scale
    terms = 2
    need = 18.5 * (top + 1.0) / 2.0
    while terms < need:
        power = jnp.dot(power, power, precision=HIGHEST, preferred_element_type=F32)
        inverse = inverse + jnp.dot(inverse, power, precision=HIGHEST, preferred_element_type=F32)
        terms *= 2
    combos = LAGS * dates
    key = first + dates * (second - first - 1)
    combo = lax.broadcasted_iota(jnp.int32, (pair_total, combos), 1)
    count = jnp.sum((combo == key).astype(F32), axis=0, keepdims=True)
    combo = lax.broadcasted_iota(jnp.int32, (dates, combos), 1)
    lag = jnp.ones_like(combo)
    for step in range(1, LAGS):
        lag = lag + (combo >= step * dates).astype(jnp.int32)
    start = combo - dates * (lag - 1)
    date = lax.broadcasted_iota(jnp.int32, (dates, combos), 0)
    spread = ((date == start).astype(F32) - (date == start + lag).astype(F32)) * count
    return jnp.dot(inverse, spread, precision=HIGHEST, preferred_element_type=F32)


def exchange_kernel(
    n, slc, rims, pairs, images, rims_out, weights, send_sem, recv_sem, rim_send, rim_recv, own_sem
):
    band = lax.axis_index("band")
    me = lax.axis_index("gx")
    date_dev = slc.shape[0]
    strip = images.shape[3]
    greet_all(n, band, me)

    def tile_copy(k, source):
        peer = lax.rem(me + k, n)
        return pltpu.make_async_remote_copy(
            src_ref=slc.at[:, :, :, pl.ds(pl.multiple_of(peer * strip, strip), strip)],
            dst_ref=images.at[pl.ds(source * date_dev, date_dev)],
            send_sem=send_sem.at[k],
            recv_sem=recv_sem.at[k],
            device_id=(band, peer),
            device_id_type=MESH,
        )

    def rim_copy(k, source):
        peer = lax.rem(me + k, n)
        return pltpu.make_async_remote_copy(
            src_ref=rims.at[peer],
            dst_ref=rims_out.at[source],
            send_sem=rim_send.at[k],
            recv_sem=rim_recv.at[k],
            device_id=(band, peer),
            device_id_type=MESH,
        )

    def start(k, carry):
        tile_copy(k, me).start()
        rim_copy(k, me).start()
        return carry

    lax.fori_loop(1, n, start, 0)
    own_tile = pltpu.make_async_copy(
        slc.at[:, :, :, pl.ds(pl.multiple_of(me * strip, strip), strip)],
        images.at[pl.ds(me * date_dev, date_dev)],
        own_sem.at[0],
    )
    own_rim = pltpu.make_async_copy(rims.at[me], rims_out.at[me], own_sem.at[1])
    own_tile.start()
    own_rim.start()
    dates = date_dev * n
    weights[...] = network_weights(pairs[...], dates, 2.0 * (pairs.shape[0] // n))

    def finish(k, carry):
        source = lax.rem(me + n - k, n)
        tile = tile_copy(k, source)
        tile.wait_send()
        tile.wait_recv()
        rim = rim_copy(k, source)
        rim.wait_send()
        rim.wait_recv()
        return carry

    lax.fori_loop(1, n, finish, 0)
    own_tile.wait()
    own_rim.wait()


def split(values):
    high = values.astype(BF16)
    low = (values - high.astype(F32)).astype(BF16)
    return high, low


def cross(planes, first, second, rows):
    first = pl.ds(first, rows)
    second = pl.ds(second, rows)
    return planes[3, first, :] * planes[0, second, :] - planes[2, first, :] * planes[1, second, :]


def power(planes, first, rows):
    first = pl.ds(first, rows)
    return planes[2, first, :] * planes[0, first, :] + planes[3, first, :] * planes[1, first, :]


def strip_kernel(
    images, rims, weight, rim_weight, weights, columns, series, sums, planes, rim_planes,
    high, low, rim_high, rim_low, powers, solved
):
    dates, _, rows, strip = images.shape
    pitch = dates + 8
    halves = rows // 16
    devices = rims.shape[0]
    date_dev = dates // devices
    combos = LAGS * dates
    block = 16

    zero = jnp.zeros((8, strip), F32)
    for part in range(4):
        for r in range(rows):
            planes[part, r * pitch + dates : (r + 1) * pitch, :] = zero
        for half in range(halves):
            rim_planes[part, half * pitch + dates : (half + 1) * pitch, :] = zero
    powers[dates:pitch, :] = zero

    def place(t, carry):
        for part in range(2):
            plane = images[t, part].astype(F32)
            heavy = plane * weight[...]
            for q in range(rows // 8):
                target = pl.ds(q * 8 * pitch + t, 8, stride=pitch)
                planes[part, target, :] = plane[q * 8 : q * 8 + 8]
                planes[part + 2, target, :] = heavy[q * 8 : q * 8 + 8]
        return carry

    lax.fori_loop(0, dates, place, 0, unroll=4)

    for d in range(devices):
        tile = rims[d].astype(F32)
        for part in range(2):
            for half in range(halves):
                at = (part * halves + half) * date_dev
                piece = tile[at : at + date_dev]
                target = half * pitch + d * date_dev
                rim_planes[part, target : target + date_dev, :] = piece
                rim_planes[part + 2, target : target + date_dev, :] = (
                    piece * rim_weight[half : half + 1, :]
                )

    def row_sums(b, carry):
        t0 = pl.multiple_of(b * block, block)
        for lag in range(LAGS + 1):
            ones, twos, fours, eights = {}, {}, {}, {}

            def emit(r):
                total = eights.get(r - RIM)
                if r + RIM < rows:
                    total = total + ones[r + RIM]
                h, l = split(total)
                where = pl.ds(pl.multiple_of(lag * dates + t0, block), block)
                high[r, where, :] = h
                low[r, where, :] = l

            for r in range(rows):
                if lag == 0:
                    ones[r] = power(planes, r * pitch + t0, block)
                else:
                    ones[r] = cross(planes, r * pitch + t0, r * pitch + t0 + lag, block)
                twos[r - 1] = ones[r - 1] + ones[r] if r >= 1 else ones[r]
                fours[r - 3] = twos[r - 3] + twos[r - 1] if r >= 2 else twos[r - 1]
                eights[r - 7] = fours[r - 7] + fours[r - 3] if r >= 4 else fours[r - 3]
                if r >= RIM:
                    emit(r - RIM)
            twos[rows - 1] = ones[rows - 1]
            for s in range(rows - 3, rows):
                fours[s] = twos[s] + twos[s + 2] if s + 2 < rows else twos[s]
            for s in range(rows - 7, rows - 4):
                eights[s] = fours[s] + fours[s + 4]
            for r in range(rows - RIM, rows):
                emit(r)
        return carry

    lax.fori_loop(0, dates // block, row_sums, 0)

    pieces = []
    for lag in range(LAGS + 1):
        line = []
        for half in range(halves):
            if lag == 0:
                line.append(power(rim_planes, half * pitch, dates))
            else:
                line.append(cross(rim_planes, half * pitch, half * pitch + lag, dates))
        pieces.append(jnp.concatenate(line, axis=1))
    rim_all = jnp.concatenate(pieces, axis=0)
    lanes = rows * 8
    a = lax.broadcasted_iota(jnp.int32, (lanes, lanes), 0)
    b = lax.broadcasted_iota(jnp.int32, (lanes, lanes), 1)
    near = (jnp.abs((a >> 3) - (b >> 3)) <= RIM) & ((a & 7) == (b & 7))
    near = jnp.where(near, 1.0, 0.0).astype(BF16)
    h, l = split(rim_all)
    rim_sum = jnp.dot(h, near, preferred_element_type=F32) + jnp.dot(
        l, near, preferred_element_type=F32
    )
    h, l = split(rim_sum)
    for half in range(halves):
        rim_high[half] = h[:, half * 128 : half * 128 + 128]
        rim_low[half] = l[:, half * 128 : half * 128 + 128]

    k = lax.broadcasted_iota(jnp.int32, (strip, strip), 0)
    c = lax.broadcasted_iota(jnp.int32, (strip, strip), 1)
    main = jnp.where(jnp.abs(k - c) <= RIM, 1.0, 0.0).astype(BF16)
    k = lax.broadcasted_iota(jnp.int32, (128, strip), 0)
    c = lax.broadcasted_iota(jnp.int32, (128, strip), 1)
    offset = k & 7
    place_col = jnp.where(offset < RIM, offset - RIM, strip + offset - RIM)
    rim_near = jnp.where(jnp.abs(place_col - c) <= RIM, 1.0, 0.0)
    w_high, w_low = split(weights[...])
    mix = jnp.concatenate([w_high, w_low], axis=0)

    def one_row(r, total):
        half = lax.div(r, 16)
        within = lax.rem(r, 16)
        side = jnp.where((k >> 3) == within, rim_near, 0.0).astype(BF16)
        band_matrix = jnp.concatenate([main, side], axis=0)
        looked = jnp.dot(
            jnp.concatenate([high[r], rim_high[half]], axis=1),
            band_matrix,
            preferred_element_type=F32,
        ) + jnp.dot(
            jnp.concatenate([low[r], rim_low[half]], axis=1),
            band_matrix,
            preferred_element_type=F32,
        )
        first = looked[0:dates]
        powers[0:dates, :] = first
        observed = []
        for lag in range(1, LAGS + 1):
            second = powers[lag : lag + dates, :]
            sine = looked[lag * dates : (lag + 1) * dates] * lax.rsqrt(first * second + 1e-6)
            observed.append(sine.astype(BF16))
        both = jnp.dot(mix, jnp.concatenate(observed, axis=0), preferred_element_type=F32)
        value = both[0:dates] + both[dates:]
        solved[pl.ds(pl.multiple_of(r * dates, dates), dates), :] = value
        return total + value

    total = lax.fori_loop(0, rows, one_row, jnp.zeros((dates, strip), F32))
    mean = jnp.sum(total, axis=1, keepdims=True)
    slope = jnp.sum(total * columns[...], axis=1, keepdims=True)
    lane = lax.broadcasted_iota(jnp.int32, (dates, 128), 1)
    sums[...] = jnp.where(lane == 0, mean, slope).T[0:8]

    def unplace(t, carry):
        for q in range(rows // 8):
            series[t, q * 8 : q * 8 + 8, :] = solved[pl.ds(q * 8 * dates + t, 8, stride=dates), :]
        return carry

    lax.fori_loop(0, dates, unplace, 0, unroll=8)


def total_kernel(n, mine, total, slots, send_sem, recv_sem):
    band = lax.axis_index("band")
    me = lax.axis_index("gx")
    greet_all(n, band, me)

    def copy(k, source):
        return pltpu.make_async_remote_copy(
            src_ref=mine,
            dst_ref=slots.at[source],
            send_sem=send_sem.at[k],
            recv_sem=recv_sem.at[k],
            device_id=(band, lax.rem(me + k, n)),
            device_id_type=MESH,
        )

    def start(k, carry):
        copy(k, me).start()
        return carry

    def finish(k, carry):
        one = copy(k, lax.rem(me + n - k, n))
        one.wait_send()
        one.wait_recv()
        return carry

    lax.fori_loop(1, n, start, 0)
    slots[me] = mine[...]
    lax.fori_loop(1, n, finish, 0)
    total[...] = lax.fori_loop(1, n, lambda k, acc: acc + slots[k], slots[0])


def rim_lanes(values, strip):
    lead = values.shape[:-2]
    rows, cols = values.shape[-2:]
    strips = cols // strip
    view = values.reshape(lead + (rows, strips, strip))
    left = view[..., strip - RIM :]
    right = view[..., :RIM]
    gap = jnp.zeros(lead + (rows, 1, RIM), values.dtype)
    left = jnp.concatenate([gap, left[..., :-1, :]], axis=-2)
    right = jnp.concatenate([right[..., 1:, :], gap], axis=-2)
    both = jnp.concatenate([left, right], axis=-1)
    both = jnp.moveaxis(both, -2, 0)
    return both.reshape((strips,) + lead + (rows // 16, 128))


def body(slc_tiles, look_weight, pair_list):
    n = lax.axis_size("gx")
    me = lax.axis_index("gx")
    date_dev, _, rows, cols = slc_tiles.shape
    strip = cols // n
    dates = date_dev * n
    pitch = dates + 8
    halves = rows // 16
    combos = LAGS * dates
    planned = (LAGS + 1) * dates

    rims = rim_lanes(slc_tiles, strip)
    rims = jnp.transpose(rims, (0, 2, 3, 1, 4)).reshape(n, 2 * halves * date_dev, 128)
    weight = lax.dynamic_slice_in_dim(look_weight, me * strip, strip, 1)
    rim_weight = lax.dynamic_index_in_dim(rim_lanes(look_weight, strip), me, 0, keepdims=False)

    vmem = pl.BlockSpec(memory_space=pltpu.VMEM)
    anywhere = pl.BlockSpec(memory_space=pl.ANY)
    dma = pltpu.SemaphoreType.DMA
    images, rims, weights = pl.pallas_call(
        functools.partial(exchange_kernel, n),
        out_shape=(
            jax.ShapeDtypeStruct((dates, 2, rows, strip), BF16),
            jax.ShapeDtypeStruct(rims.shape, BF16),
            jax.ShapeDtypeStruct((dates, combos), F32),
        ),
        in_specs=[anywhere, anywhere, vmem],
        out_specs=(anywhere, anywhere, vmem),
        scratch_shapes=[dma((n,)), dma((n,)), dma((n,)), dma((n,)), dma((2,))],
        compiler_params=pltpu.CompilerParams(
            collective_id=0, has_side_effects=True, vmem_limit_bytes=48 * MIB
        ),
    )(slc_tiles, rims, pair_list)

    column_ids = me * strip + lax.iota(jnp.int32, strip)
    columns = (2.0 * column_ids.astype(F32) + 1.0) / cols - 1.0
    series, sums = pl.pallas_call(
        strip_kernel,
        out_shape=(
            jax.ShapeDtypeStruct((dates, rows, strip), F32),
            jax.ShapeDtypeStruct((8, dates), F32),
        ),
        in_specs=[vmem] * 6,
        out_specs=(vmem, vmem),
        scratch_shapes=[
            pltpu.VMEM((4, rows * pitch, strip), F32),
            pltpu.VMEM((4, halves * pitch, 128), F32),
            pltpu.VMEM((rows, planned, strip), BF16),
            pltpu.VMEM((rows, planned, strip), BF16),
            pltpu.VMEM((halves, planned, 128), BF16),
            pltpu.VMEM((halves, planned, 128), BF16),
            pltpu.VMEM((pitch, strip), F32),
            pltpu.VMEM((rows * dates, strip), F32),
        ],
        compiler_params=pltpu.CompilerParams(vmem_limit_bytes=60 * MIB),
    )(images, rims, weight, rim_weight, weights, columns[None, :])

    totals = pl.pallas_call(
        functools.partial(total_kernel, n),
        out_shape=jax.ShapeDtypeStruct((8, dates), F32),
        in_specs=[vmem],
        out_specs=vmem,
        scratch_shapes=[pltpu.VMEM((n, 8, dates), F32), dma((n,)), dma((n,))],
        compiler_params=pltpu.CompilerParams(collective_id=1, has_side_effects=True),
    )(sums)

    all_cols = (2.0 * lax.iota(jnp.int32, cols).astype(F32) + 1.0) / cols - 1.0
    square_sum = jnp.sum(all_cols * all_cols)
    date_mean = totals[0] / (rows * cols)
    date_slope = totals[1] / (rows * square_sum)
    return series - date_mean[:, None, None] - date_slope[:, None, None] * columns


def solution(mesh):
    return jax.shard_map(
        body,
        mesh=mesh,
        in_specs=(P("gx", None, "band", None), P("band", None), P()),
        out_specs=P(None, "band", "gx"),
        check_vma=False,
    )
```

```python
import functools
import math

import jax
import jax.numpy as jnp
from jax import lax
from jax.experimental import pallas as pl
from jax.experimental.pallas import tpu as pltpu
from jax.sharding import PartitionSpec as P

LOOK = 9
RIM = LOOK // 2
LAGS = 4
MESH = pl.DeviceIdType.MESH
F32 = jnp.float32
BF16 = jnp.bfloat16
HIGHEST = lax.Precision.HIGHEST
MIB = 1024 * 1024


def greet_all(n, band, me):
    barrier = pltpu.get_barrier_semaphore()

    def greet(k, carry):
        peer = lax.rem(me + k, n)
        pl.semaphore_signal(barrier, inc=1, device_id=(band, peer), device_id_type=MESH)
        return carry

    lax.fori_loop(1, n, greet, 0)
    pl.semaphore_wait(barrier, n - 1)


def network_weights(pairs, dates, degree_bound):
    pair_total = pairs.shape[0]
    first = pairs[:, 0:1]
    second = pairs[:, 1:2]
    ids = lax.broadcasted_iota(jnp.int32, (pair_total, dates), 1)
    incidence_t = (ids == first).astype(F32) - (ids == second).astype(F32)
    incidence = incidence_t.T
    product = jnp.dot(incidence.astype(BF16), incidence_t.astype(BF16), preferred_element_type=F32)
    row = lax.broadcasted_iota(jnp.int32, (dates, dates), 0)
    col = lax.broadcasted_iota(jnp.int32, (dates, dates), 1)
    eye = (row == col).astype(F32)
    normal = product + eye
    top = 1.0 + 2.0 * degree_bound
    scale = 2.0 / (1.0 + top)
    power = eye - normal * scale
    inverse = (eye + power) * scale
    terms = 2
    need = 18.5 * (top + 1.0) / 2.0
    while terms < need:
        power = jnp.dot(power, power, precision=HIGHEST, preferred_element_type=F32)
        inverse = inverse + jnp.dot(inverse, power, precision=HIGHEST, preferred_element_type=F32)
        terms *= 2
    combos = LAGS * dates
    key = first + dates * (second - first - 1)
    combo = lax.broadcasted_iota(jnp.int32, (pair_total, combos), 1)
    count = jnp.sum((combo == key).astype(F32), axis=0, keepdims=True)
    combo = lax.broadcasted_iota(jnp.int32, (dates, combos), 1)
    lag = jnp.ones_like(combo)
    for step in range(1, LAGS):
        lag = lag + (combo >= step * dates).astype(jnp.int32)
    start = combo - dates * (lag - 1)
    date = lax.broadcasted_iota(jnp.int32, (dates, combos), 0)
    spread = ((date == start).astype(F32) - (date == start + lag).astype(F32)) * count
    return jnp.dot(inverse, spread, precision=HIGHEST, preferred_element_type=F32)


def split(values):
    high = values.astype(BF16)
    low = (values - high.astype(F32)).astype(BF16)
    return high, low


def cross(planes, first, second, rows):
    first = pl.ds(first, rows)
    second = pl.ds(second, rows)
    return planes[3, first, :] * planes[0, second, :] - planes[2, first, :] * planes[1, second, :]


def power(planes, first, rows):
    first = pl.ds(first, rows)
    return planes[2, first, :] * planes[0, first, :] + planes[3, first, :] * planes[1, first, :]


def window_sums(term, lo, hi, out_lo, out_hi):
    @functools.cache
    def ones(r):
        return term(r) if lo <= r < hi else None

    @functools.cache
    def run(r, size):
        if size == 1:
            return ones(r)
        a, b = run(r, size // 2), run(r + size // 2, size // 2)
        return b if a is None else a if b is None else a + b

    for r in range(out_lo, out_hi):
        total, last = run(r - RIM, LOOK - 1), ones(r + RIM)
        yield r, total if last is None else total + last


def kernel(
    n, slc, look_weight, pairs, series,
    local, images, rim_parts, rim_send, rim_recv, weight, weights, planes, rim_planes,
    high, low, rim_high, rim_low, powers, solved, mine, slots, trend,
    send_sem, recv_sem, own_sem,
):
    band = lax.axis_index("band")
    me = lax.axis_index("gx")
    date_dev, _, rows, cols = slc.shape
    halves, dates, _, block, strip = images.shape
    pitch = dates + 8
    groups = date_dev * 2 * halves

    def columns_of(j):
        return pl.ds(pl.multiple_of(j * strip, strip), strip)

    fetch = pltpu.make_async_copy(slc, local, own_sem.at[0])
    fetch.start()
    sides = (lax.max(me - 1, 0), me, lax.min(me + 1, n - 1))
    weight_copies = [
        pltpu.make_async_copy(look_weight.at[:, columns_of(j)], weight.at[i], own_sem.at[1 + i])
        for i, j in enumerate(sides)
    ]
    for copy in weight_copies:
        copy.start()
    own_tiles = [
        pltpu.make_async_copy(
            slc.at[:, :, pl.ds(h * block, block), columns_of(me)],
            images.at[h, pl.ds(me * date_dev, date_dev)],
            own_sem.at[4 + h],
        )
        for h in range(halves)
    ]
    for copy in own_tiles:
        copy.start()
    greet_all(n, band, me)

    def tile_copy(h, k, source):
        peer = lax.rem(me + k, n)
        return pltpu.make_async_remote_copy(
            src_ref=slc.at[:, :, pl.ds(h * block, block), columns_of(peer)],
            dst_ref=images.at[h, pl.ds(source * date_dev, date_dev)],
            send_sem=send_sem.at[h, k],
            recv_sem=recv_sem.at[h, k],
            device_id=(band, peer),
            device_id_type=MESH,
        )

    def rim_copy(k, source):
        peer = lax.rem(me + k, n)
        return pltpu.make_async_remote_copy(
            src_ref=rim_send.at[peer],
            dst_ref=rim_recv.at[source],
            send_sem=send_sem.at[halves, k],
            recv_sem=recv_sem.at[halves, k],
            device_id=(band, peer),
            device_id_type=MESH,
        )

    def sum_copy(k, source):
        return pltpu.make_async_remote_copy(
            src_ref=mine,
            dst_ref=slots.at[source],
            send_sem=send_sem.at[halves + 1, k],
            recv_sem=recv_sem.at[halves + 1, k],
            device_id=(band, lax.rem(me + k, n)),
            device_id_type=MESH,
        )

    def start_all(make):
        def start(k, carry):
            make(k, me).start()
            return carry

        lax.fori_loop(1, n, start, 0)

    def finish_all(make):
        def finish(k, carry):
            one = make(k, lax.rem(me + n - k, n))
            one.wait_send()
            one.wait_recv()
            return carry

        lax.fori_loop(1, n, finish, 0)

    start_all(functools.partial(tile_copy, 0))

    a = lax.broadcasted_iota(jnp.int32, (strip, 256), 0)
    b = lax.broadcasted_iota(jnp.int32, (strip, 256), 1)
    h = b & 7
    pick = ((b < 128) & (h < RIM) & (a == strip - RIM + h)) | (
        (b >= 128) & (h >= RIM) & (a == h - RIM)
    )
    pick = jnp.where(pick, 1.0, 0.0)
    pick_half = pick.astype(BF16)
    tall = groups * block
    a = lax.broadcasted_iota(jnp.int32, (tall, 256), 0)
    b = lax.broadcasted_iota(jnp.int32, (tall, 256), 1)
    keep = jnp.where((a & (block - 1)) == ((b & 127) >> 3), 1.0, 0.0)
    a = lax.broadcasted_iota(jnp.int32, (groups, tall), 0)
    b = lax.broadcasted_iota(jnp.int32, (groups, tall), 1) >> 4
    gather = jnp.zeros((groups, tall), jnp.bool_)
    for d in range(date_dev):
        for ph in range(2 * halves):
            gather = gather | ((b == d * 2 * halves + ph) & (a == ph * date_dev + d))
    gather = jnp.where(gather, 1.0, 0.0).astype(BF16)
    empty = jnp.zeros((groups, 256), F32)
    rim_parts[0] = empty
    rim_parts[n + 1] = empty
    fetch.wait()

    def pick_rims(j, carry):
        slab = local[:, :, :, columns_of(j)].reshape(tall, strip)
        spread = jnp.dot(slab, pick_half, preferred_element_type=F32) * keep
        rim_parts[j + 1] = jnp.dot(gather, spread.astype(BF16), preferred_element_type=F32)
        return carry

    lax.fori_loop(0, n, pick_rims, 0)

    def join_rims(j, carry):
        rim_send[j] = (rim_parts[j, :, 0:128] + rim_parts[j + 2, :, 128:256]).astype(BF16)
        return carry

    lax.fori_loop(0, n, join_rims, 0)
    start_all(rim_copy)
    for half in range(1, halves):
        start_all(functools.partial(tile_copy, half))
    rim_recv[me] = rim_send[me]

    weights[...] = network_weights(pairs[...], dates, 2.0 * (pairs.shape[0] // n))
    w_high, w_low = split(weights[...])
    mix = jnp.concatenate([w_high, w_low], axis=0)
    column_ids = me * strip + lax.broadcasted_iota(jnp.int32, (1, strip), 1)
    columns = (2.0 * column_ids.astype(F32) + 1.0) / cols - 1.0

    for copy in weight_copies:
        copy.wait()
    rim_weight = jnp.dot(
        weight[0], pick[:, 0:128], precision=HIGHEST, preferred_element_type=F32
    ) + jnp.dot(weight[2], pick[:, 128:256], precision=HIGHEST, preferred_element_type=F32)

    zero = jnp.zeros((8, strip), F32)
    for part in range(4):
        for r in range(rows):
            planes[part, r * pitch + dates : (r + 1) * pitch, :] = zero
        for half in range(halves):
            rim_planes[part, half * pitch + dates : (half + 1) * pitch, :] = zero
    for slot in range(powers.shape[0]):
        powers[slot, dates:pitch, :] = zero

    def place_half(half):
        def place(t, carry):
            for part in range(2):
                plane = images[half, t, part].astype(F32)
                heavy = plane * weight[1, half * block : half * block + block, :]
                for q in range(block // 8):
                    row = half * block + q * 8
                    target = pl.ds(row * pitch + t, 8, stride=pitch)
                    planes[part, target, :] = plane[q * 8 : q * 8 + 8]
                    planes[part + 2, target, :] = heavy[q * 8 : q * 8 + 8]
            return carry

        lax.fori_loop(0, dates, place, 0, unroll=4)

    k = lax.broadcasted_iota(jnp.int32, (strip, strip), 0)
    c = lax.broadcasted_iota(jnp.int32, (strip, strip), 1)
    main = jnp.where(jnp.abs(k - c) <= RIM, 1.0, 0.0).astype(BF16)
    k = lax.broadcasted_iota(jnp.int32, (128, strip), 0)
    c = lax.broadcasted_iota(jnp.int32, (128, strip), 1)
    offset = k & 7
    rim_col = jnp.where(offset < RIM, offset - RIM, strip + offset - RIM)
    rim_near = jnp.where(jnp.abs(rim_col - c) <= RIM, 1.0, 0.0)
    together = powers.shape[0]

    def stage(lo, hi, out_lo, out_hi, total):
        def row_sums(b, carry):
            t0 = pl.multiple_of(b * block, block)
            for lag in range(LAGS + 1):
                where = pl.ds(pl.multiple_of(lag * dates + t0, block), block)

                def term(r):
                    first = r * pitch + t0
                    if lag == 0:
                        return power(planes, first, block)
                    return cross(planes, first, first + lag, block)

                for r, value in window_sums(term, lo, hi, out_lo, out_hi):
                    h, l = split(value)
                    high[r - out_lo, where, :] = h
                    low[r - out_lo, where, :] = l
            return carry

        lax.fori_loop(0, dates // block, row_sums, 0)

        def some_rows(g, total):
            looks = []
            for i in range(together):
                at = g * together + i
                r = at + out_lo
                half = lax.div(r, block)
                side = jnp.where((k >> 3) == lax.rem(r, block), rim_near, 0.0).astype(BF16)
                matrix = jnp.concatenate([main, side], axis=0)
                looked = jnp.dot(
                    jnp.concatenate([high[at], rim_high[half]], axis=1),
                    matrix,
                    preferred_element_type=F32,
                ) + jnp.dot(
                    jnp.concatenate([low[at], rim_low[half]], axis=1),
                    matrix,
                    preferred_element_type=F32,
                )
                powers[i, 0:dates, :] = looked[0:dates]
                looks.append(looked)
            sines = []
            for i in range(together):
                looked = looks[i]
                observed = []
                for lag in range(1, LAGS + 1):
                    both = looked[0:dates] * powers[i, lag : lag + dates, :]
                    sine = looked[lag * dates : (lag + 1) * dates] * lax.rsqrt(both + 1e-6)
                    observed.append(sine.astype(BF16))
                sines.append(jnp.concatenate(observed, axis=0))
            for i in range(0, together, 2):
                pair = jnp.concatenate(sines[i : i + 2], axis=1)
                both = jnp.dot(mix, pair, preferred_element_type=F32)
                value = both[0:dates] + both[dates:]
                for e in range(2):
                    r = g * together + i + e + out_lo
                    one = value[:, e * strip : (e + 1) * strip]
                    solved[pl.ds(pl.multiple_of(r * dates, dates), dates), :] = one
                    total = total + one
            return total

        return lax.fori_loop(0, (out_hi - out_lo) // together, some_rows, total)

    finish_all(functools.partial(tile_copy, 0))
    own_tiles[0].wait()
    place_half(0)
    finish_all(rim_copy)

    a = lax.broadcasted_iota(jnp.int32, (rows, 128), 0)
    b = lax.broadcasted_iota(jnp.int32, (rows, 128), 1)
    rim_weight = jnp.where((a & (block - 1)) == (b >> 3), rim_weight, 0.0)
    for half in range(halves):
        heavy = jnp.sum(rim_weight[half * block : half * block + block], axis=0, keepdims=True)
        for d in range(n):
            for part in range(2):
                at = (part * halves + half) * date_dev
                piece = rim_recv[d].astype(F32)[at : at + date_dev]
                target = half * pitch + d * date_dev
                rim_planes[part, target : target + date_dev, :] = piece
                rim_planes[part + 2, target : target + date_dev, :] = piece * heavy
    pieces = []
    for lag in range(LAGS + 1):
        line = []
        for half in range(halves):
            if lag == 0:
                line.append(power(rim_planes, half * pitch, dates))
            else:
                line.append(cross(rim_planes, half * pitch, half * pitch + lag, dates))
        pieces.append(jnp.concatenate(line, axis=1))
    lanes = rows * 8
    a = lax.broadcasted_iota(jnp.int32, (lanes, lanes), 0)
    b = lax.broadcasted_iota(jnp.int32, (lanes, lanes), 1)
    near = (jnp.abs((a >> 3) - (b >> 3)) <= RIM) & ((a & 7) == (b & 7))
    near = jnp.where(near, 1.0, 0.0).astype(BF16)
    h, l = split(jnp.concatenate(pieces, axis=0))
    rim_sum = jnp.dot(h, near, preferred_element_type=F32) + jnp.dot(
        l, near, preferred_element_type=F32
    )
    h, l = split(rim_sum)
    for half in range(halves):
        rim_high[half] = h[:, half * 128 : half * 128 + 128]
        rim_low[half] = l[:, half * 128 : half * 128 + 128]

    total = jnp.zeros((dates, strip), F32)
    ready = block - RIM
    total = stage(0, block, 0, ready, total)
    for half in range(1, halves):
        finish_all(functools.partial(tile_copy, half))
        own_tiles[half].wait()
        place_half(half)
    total = stage(ready - RIM, rows, ready, rows, total)

    mean = jnp.sum(total, axis=1, keepdims=True)
    slope = jnp.sum(total * columns, axis=1, keepdims=True)
    lane = lax.broadcasted_iota(jnp.int32, (dates, 128), 1)
    mine[...] = jnp.where(lane == 0, mean, slope).T[0:8]
    start_all(sum_copy)
    slots[me] = mine[...]
    all_cols = lax.broadcasted_iota(jnp.int32, (1, cols), 1)
    all_cols = (2.0 * all_cols.astype(F32) + 1.0) / cols - 1.0
    square_sum = jnp.sum(all_cols * all_cols, axis=1, keepdims=True)
    finish_all(sum_copy)
    sums = lax.fori_loop(1, n, lambda s, acc: acc + slots[s], slots[0]).T
    date_mean = sums[:, 0:1] / (rows * cols)
    date_slope = sums[:, 1:2] / (rows * square_sum)
    trend[...] = date_mean + date_slope * columns

    def unplace(t, carry):
        gone = trend[pl.ds(t, 1), :]
        for q in range(rows // 8):
            piece = solved[pl.ds(q * 8 * dates + t, 8, stride=dates), :]
            series[t, q * 8 : q * 8 + 8, :] = piece - gone
        return carry

    lax.fori_loop(0, dates, unplace, 0, unroll=8)


def body(slc_tiles, look_weight, pair_list):
    n = lax.axis_size("gx")
    date_dev, _, rows, cols = slc_tiles.shape
    block = 16
    strip = cols // n
    dates = date_dev * n
    pitch = dates + 8
    halves = rows // block
    planned = (LAGS + 1) * dates
    most = rows - block + RIM
    lines = 2 * halves * date_dev

    vmem = pl.BlockSpec(memory_space=pltpu.VMEM)
    anywhere = pl.BlockSpec(memory_space=pl.ANY)
    dma = pltpu.SemaphoreType.DMA
    return pl.pallas_call(
        functools.partial(kernel, n),
        out_shape=jax.ShapeDtypeStruct((dates, rows, strip), F32),
        in_specs=[anywhere, anywhere, vmem],
        out_specs=vmem,
        scratch_shapes=[
            pltpu.VMEM(slc_tiles.shape, BF16),
            pltpu.VMEM((halves, dates, 2, block, strip), BF16),
            pltpu.VMEM((n + 2, lines, 256), F32),
            pltpu.VMEM((n, lines, 128), BF16),
            pltpu.VMEM((n, lines, 128), BF16),
            pltpu.VMEM((3, rows, strip), F32),
            pltpu.VMEM((dates, LAGS * dates), F32),
            pltpu.VMEM((4, rows * pitch, strip), F32),
            pltpu.VMEM((4, halves * pitch, 128), F32),
            pltpu.VMEM((most, planned, strip), BF16),
            pltpu.VMEM((most, planned, strip), BF16),
            pltpu.VMEM((halves, planned, 128), BF16),
            pltpu.VMEM((halves, planned, 128), BF16),
            pltpu.VMEM((4, pitch, strip), F32),
            pltpu.VMEM((rows * dates, strip), F32),
            pltpu.VMEM((8, dates), F32),
            pltpu.VMEM((n, 8, dates), F32),
            pltpu.VMEM((dates, strip), F32),
            dma((halves + 2, n)),
            dma((halves + 2, n)),
            dma((4 + halves,)),
        ],
        compiler_params=pltpu.CompilerParams(
            collective_id=0, has_side_effects=True, vmem_limit_bytes=60 * MIB
        ),
    )(slc_tiles, look_weight, pair_list)


def solution(mesh):
    return jax.shard_map(
        body,
        mesh=mesh,
        in_specs=(P("gx", None, "band", None), P("band", None), P()),
        out_specs=P(None, "band", "gx"),
        check_vma=False,
    )
```

```python
import functools
import math

import jax
import jax.numpy as jnp
from jax import lax
from jax.experimental import pallas as pl
from jax.experimental.pallas import tpu as pltpu
from jax.sharding import PartitionSpec as P

LOOK = 9
RIM = LOOK // 2
LAGS = 4
MESH = pl.DeviceIdType.MESH
F32 = jnp.float32
BF16 = jnp.bfloat16
HIGHEST = lax.Precision.HIGHEST
MIB = 1024 * 1024


def greet_all(n, band, me):
    barrier = pltpu.get_barrier_semaphore()

    def greet(k, carry):
        peer = lax.rem(me + k, n)
        pl.semaphore_signal(barrier, inc=1, device_id=(band, peer), device_id_type=MESH)
        return carry

    lax.fori_loop(1, n, greet, 0)
    pl.semaphore_wait(barrier, n - 1)


def network_weights(pairs, dates, degree_bound):
    pair_total = pairs.shape[1]
    first = pairs[0:1]
    second = pairs[1:2]
    ids = lax.broadcasted_iota(jnp.int32, (dates, pair_total), 0)
    incidence = (ids == first).astype(F32) - (ids == second).astype(F32)
    incidence_t = incidence.T
    product = jnp.dot(incidence.astype(BF16), incidence_t.astype(BF16), preferred_element_type=F32)
    row = lax.broadcasted_iota(jnp.int32, (dates, dates), 0)
    col = lax.broadcasted_iota(jnp.int32, (dates, dates), 1)
    eye = (row == col).astype(F32)
    normal = product + eye
    top = 1.0 + 2.0 * degree_bound
    scale = 2.0 / (1.0 + top)
    power = eye - normal * scale
    inverse = (eye + power) * scale
    terms = 2
    need = 18.5 * (top + 1.0) / 2.0
    while terms < need:
        power = jnp.dot(power, power, precision=HIGHEST, preferred_element_type=F32)
        inverse = inverse + jnp.dot(inverse, power, precision=HIGHEST, preferred_element_type=F32)
        terms *= 2
    combos = LAGS * dates
    key = (first + dates * (second - first - 1)).astype(F32)
    key = jnp.broadcast_to(key, (8, pair_total)).T[:, 0:1].astype(jnp.int32)
    combo = lax.broadcasted_iota(jnp.int32, (pair_total, combos), 1)
    count = jnp.sum((combo == key).astype(F32), axis=0, keepdims=True)
    combo = lax.broadcasted_iota(jnp.int32, (dates, combos), 1)
    lag = jnp.ones_like(combo)
    for step in range(1, LAGS):
        lag = lag + (combo >= step * dates).astype(jnp.int32)
    start = combo - dates * (lag - 1)
    date = lax.broadcasted_iota(jnp.int32, (dates, combos), 0)
    spread = ((date == start).astype(F32) - (date == start + lag).astype(F32)) * count
    return jnp.dot(inverse, spread, precision=HIGHEST, preferred_element_type=F32)


def split(values):
    high = values.astype(BF16)
    low = (values - high.astype(F32)).astype(BF16)
    return high, low


def cross(planes, first, second, rows):
    first = pl.ds(first, rows)
    second = pl.ds(second, rows)
    return planes[3, first, :] * planes[0, second, :] - planes[2, first, :] * planes[1, second, :]


def power(planes, first, rows):
    first = pl.ds(first, rows)
    return planes[2, first, :] * planes[0, first, :] + planes[3, first, :] * planes[1, first, :]


def window_sums(term, lo, hi, out_lo, out_hi):
    @functools.cache
    def ones(r):
        return term(r) if lo <= r < hi else None

    @functools.cache
    def run(r, size):
        if size == 1:
            return ones(r)
        a, b = run(r, size // 2), run(r + size // 2, size // 2)
        return b if a is None else a if b is None else a + b

    for r in range(out_lo, out_hi):
        total, last = run(r - RIM, LOOK - 1), ones(r + RIM)
        yield r, total if last is None else total + last


def kernel(
    n, slc, look_weight, pairs, series,
    local, packed, images, rim_parts, rim_send, rim_recv, weight, weights, planes, rim_planes,
    high, low, rim_high, rim_low, powers, solved, mine, slots, trend,
    send_sem, recv_sem, own_sem,
):
    band = lax.axis_index("band")
    me = lax.axis_index("gx")
    date_dev, _, rows, cols = slc.shape
    chunks, dates, block, strip = images.shape
    halves = chunks // 2
    part_rows = block // 2
    pitch = dates + 8
    groups = date_dev * 2 * halves

    def columns_of(j):
        return pl.ds(pl.multiple_of(j * strip, strip), strip)

    fetch = pltpu.make_async_copy(slc, local, own_sem.at[0])
    fetch.start()
    sides = (lax.max(me - 1, 0), me, lax.min(me + 1, n - 1))
    weight_copies = [
        pltpu.make_async_copy(look_weight.at[:, columns_of(j)], weight.at[i], own_sem.at[1 + i])
        for i, j in enumerate(sides)
    ]
    for copy in weight_copies:
        copy.start()
    own_tiles = [
        pltpu.make_async_copy(
            packed.at[c, :, :, columns_of(me)],
            images.at[c, pl.ds(me * date_dev, date_dev)],
            own_sem.at[4 + c],
        )
        for c in range(chunks)
    ]

    def pack(half):
        for d in range(date_dev):
            real = local[d, 0, half * block : half * block + block, :].astype(F32)
            imag = local[d, 1, half * block : half * block + block, :].astype(F32)
            for e in range(2):
                at = slice(e * part_rows, (e + 1) * part_rows)
                tile = jnp.concatenate([real[at], imag[at]], axis=0)
                packed[2 * half + e, d] = tile.astype(BF16)

    fetch.wait()
    pack(0)
    greet_all(n, band, me)

    def tile_copy(c, k, source):
        peer = lax.rem(me + k, n)
        return pltpu.make_async_remote_copy(
            src_ref=packed.at[c, :, :, columns_of(peer)],
            dst_ref=images.at[c, pl.ds(source * date_dev, date_dev)],
            send_sem=send_sem.at[c, k],
            recv_sem=recv_sem.at[c, k],
            device_id=(band, peer),
            device_id_type=MESH,
        )

    def rim_copy(k, source):
        peer = lax.rem(me + k, n)
        return pltpu.make_async_remote_copy(
            src_ref=rim_send.at[peer],
            dst_ref=rim_recv.at[source],
            send_sem=send_sem.at[chunks, k],
            recv_sem=recv_sem.at[chunks, k],
            device_id=(band, peer),
            device_id_type=MESH,
        )

    def sum_copy(k, source):
        return pltpu.make_async_remote_copy(
            src_ref=mine,
            dst_ref=slots.at[source],
            send_sem=send_sem.at[chunks + 1, k],
            recv_sem=recv_sem.at[chunks + 1, k],
            device_id=(band, lax.rem(me + k, n)),
            device_id_type=MESH,
        )

    def start_all(make):
        def start(k, carry):
            make(k, me).start()
            return carry

        lax.fori_loop(1, n, start, 0)

    def finish_all(make):
        def finish(k, carry):
            one = make(k, lax.rem(me + n - k, n))
            one.wait_send()
            one.wait_recv()
            return carry

        lax.fori_loop(1, n, finish, 0)

    start_all(functools.partial(tile_copy, 0))

    a = lax.broadcasted_iota(jnp.int32, (strip, 256), 0)
    b = lax.broadcasted_iota(jnp.int32, (strip, 256), 1)
    h = b & 7
    pick = ((b < 128) & (h < RIM) & (a == strip - RIM + h)) | (
        (b >= 128) & (h >= RIM) & (a == h - RIM)
    )
    pick = jnp.where(pick, 1.0, 0.0)
    pick_half = pick.astype(BF16)
    tall = groups * block
    a = lax.broadcasted_iota(jnp.int32, (tall, 256), 0)
    b = lax.broadcasted_iota(jnp.int32, (tall, 256), 1)
    keep = jnp.where((a & (block - 1)) == ((b & 127) >> 3), 1.0, 0.0)
    a = lax.broadcasted_iota(jnp.int32, (groups, tall), 0)
    b = lax.broadcasted_iota(jnp.int32, (groups, tall), 1) >> 4
    gather = jnp.zeros((groups, tall), jnp.bool_)
    for d in range(date_dev):
        for ph in range(2 * halves):
            gather = gather | ((b == d * 2 * halves + ph) & (a == ph * date_dev + d))
    gather = jnp.where(gather, 1.0, 0.0).astype(BF16)
    empty = jnp.zeros((groups, 256), F32)
    rim_parts[0] = empty
    rim_parts[n + 1] = empty

    def pick_rims(j, carry):
        slab = local[:, :, :, columns_of(j)].reshape(tall, strip)
        spread = jnp.dot(slab, pick_half, preferred_element_type=F32) * keep
        rim_parts[j + 1] = jnp.dot(gather, spread.astype(BF16), preferred_element_type=F32)
        return carry

    lax.fori_loop(0, n, pick_rims, 0)

    def join_rims(j, carry):
        rim_send[j] = (rim_parts[j, :, 0:128] + rim_parts[j + 2, :, 128:256]).astype(BF16)
        return carry

    lax.fori_loop(0, n, join_rims, 0)
    start_all(rim_copy)
    for c in range(1, chunks):
        if c % 2 == 0:
            pack(c // 2)
        start_all(functools.partial(tile_copy, c))
    for copy in own_tiles:
        copy.start()
    rim_recv[me] = rim_send[me]

    weights[...] = network_weights(pairs[...], dates, 2.0 * (pairs.shape[1] // n))
    w_high, w_low = split(weights[...])
    mix = jnp.concatenate([w_high, w_low], axis=0)
    column_ids = me * strip + lax.broadcasted_iota(jnp.int32, (1, strip), 1)
    columns = (2.0 * column_ids.astype(F32) + 1.0) / cols - 1.0

    for copy in weight_copies:
        copy.wait()
    rim_weight = jnp.dot(
        weight[0], pick[:, 0:128], precision=HIGHEST, preferred_element_type=F32
    ) + jnp.dot(weight[2], pick[:, 128:256], precision=HIGHEST, preferred_element_type=F32)

    zero = jnp.zeros((8, strip), F32)
    for part in range(4):
        for r in range(rows):
            planes[part, r * pitch + dates : (r + 1) * pitch, :] = zero
        for half in range(halves):
            rim_planes[part, half * pitch + dates : (half + 1) * pitch, :] = zero
    for slot in range(powers.shape[0]):
        powers[slot, dates:pitch, :] = zero

    def place_chunk(chunk):
        row = chunk * part_rows

        def place(t, carry):
            tile = images[chunk, t].astype(F32)
            for part in range(2):
                plane = tile[part * part_rows : (part + 1) * part_rows]
                target = pl.ds(row * pitch + t, part_rows, stride=pitch)
                planes[part, target, :] = plane
                planes[part + 2, target, :] = plane * weight[1, row : row + part_rows, :]
            return carry

        lax.fori_loop(0, dates, place, 0, unroll=8)

    k = lax.broadcasted_iota(jnp.int32, (strip, strip), 0)
    c = lax.broadcasted_iota(jnp.int32, (strip, strip), 1)
    main = jnp.where(jnp.abs(k - c) <= RIM, 1.0, 0.0).astype(BF16)
    k = lax.broadcasted_iota(jnp.int32, (128, strip), 0)
    c = lax.broadcasted_iota(jnp.int32, (128, strip), 1)
    offset = k & 7
    rim_col = jnp.where(offset < RIM, offset - RIM, strip + offset - RIM)
    rim_near = jnp.where(jnp.abs(rim_col - c) <= RIM, 1.0, 0.0)
    together = powers.shape[0]

    def stage(lo, hi, out_lo, out_hi, total):
        def row_sums(b, carry):
            t0 = pl.multiple_of(b * block, block)
            for lag in range(LAGS + 1):
                where = pl.ds(pl.multiple_of(lag * dates + t0, block), block)

                def term(r):
                    first = r * pitch + t0
                    if lag == 0:
                        return power(planes, first, block)
                    return cross(planes, first, first + lag, block)

                for r, value in window_sums(term, lo, hi, out_lo, out_hi):
                    h, l = split(value)
                    high[r - out_lo, where, :] = h
                    low[r - out_lo, where, :] = l
            return carry

        lax.fori_loop(0, dates // block, row_sums, 0)

        def some_rows(g, total):
            looks = []
            for i in range(together):
                at = g * together + i
                r = at + out_lo
                half = lax.div(r, block)
                side = jnp.where((k >> 3) == lax.rem(r, block), rim_near, 0.0).astype(BF16)
                matrix = jnp.concatenate([main, side], axis=0)
                looked = jnp.dot(
                    jnp.concatenate([high[at], rim_high[half]], axis=1),
                    matrix,
                    preferred_element_type=F32,
                ) + jnp.dot(
                    jnp.concatenate([low[at], rim_low[half]], axis=1),
                    matrix,
                    preferred_element_type=F32,
                )
                powers[i, 0:dates, :] = looked[0:dates]
                looks.append(looked)
            sines = []
            for i in range(together):
                looked = looks[i]
                observed = []
                for lag in range(1, LAGS + 1):
                    both = looked[0:dates] * powers[i, lag : lag + dates, :]
                    sine = looked[lag * dates : (lag + 1) * dates] * lax.rsqrt(both + 1e-6)
                    observed.append(sine.astype(BF16))
                sines.append(jnp.concatenate(observed, axis=0))
            for i in range(0, together, 2):
                pair = jnp.concatenate(sines[i : i + 2], axis=1)
                both = jnp.dot(mix, pair, preferred_element_type=F32)
                value = both[0:dates] + both[dates:]
                for e in range(2):
                    r = g * together + i + e + out_lo
                    one = value[:, e * strip : (e + 1) * strip]
                    solved[pl.ds(pl.multiple_of(r * dates, dates), dates), :] = one
                    total = total + one
            return total

        return lax.fori_loop(0, (out_hi - out_lo) // together, some_rows, total)

    finish_all(functools.partial(tile_copy, 0))
    own_tiles[0].wait()
    place_chunk(0)
    finish_all(rim_copy)

    a = lax.broadcasted_iota(jnp.int32, (rows, 128), 0)
    b = lax.broadcasted_iota(jnp.int32, (rows, 128), 1)
    rim_weight = jnp.where((a & (block - 1)) == (b >> 3), rim_weight, 0.0)
    for half in range(halves):
        heavy = jnp.sum(rim_weight[half * block : half * block + block], axis=0, keepdims=True)
        for d in range(n):
            for part in range(2):
                at = (part * halves + half) * date_dev
                piece = rim_recv[d].astype(F32)[at : at + date_dev]
                target = half * pitch + d * date_dev
                rim_planes[part, target : target + date_dev, :] = piece
                rim_planes[part + 2, target : target + date_dev, :] = piece * heavy
    pieces = []
    for lag in range(LAGS + 1):
        line = []
        for half in range(halves):
            if lag == 0:
                line.append(power(rim_planes, half * pitch, dates))
            else:
                line.append(cross(rim_planes, half * pitch, half * pitch + lag, dates))
        pieces.append(jnp.concatenate(line, axis=1))
    lanes = rows * 8
    a = lax.broadcasted_iota(jnp.int32, (lanes, lanes), 0)
    b = lax.broadcasted_iota(jnp.int32, (lanes, lanes), 1)
    near = (jnp.abs((a >> 3) - (b >> 3)) <= RIM) & ((a & 7) == (b & 7))
    near = jnp.where(near, 1.0, 0.0).astype(BF16)
    h, l = split(jnp.concatenate(pieces, axis=0))
    rim_sum = jnp.dot(h, near, preferred_element_type=F32) + jnp.dot(
        l, near, preferred_element_type=F32
    )
    h, l = split(rim_sum)
    for half in range(halves):
        rim_high[half] = h[:, half * 128 : half * 128 + 128]
        rim_low[half] = l[:, half * 128 : half * 128 + 128]

    total = jnp.zeros((dates, strip), F32)
    done = 0
    for c in range(chunks):
        if c > 0:
            finish_all(functools.partial(tile_copy, c))
            own_tiles[c].wait()
            place_chunk(c)
        arrived = (c + 1) * part_rows
        ready = rows if c == chunks - 1 else arrived - RIM
        total = stage(max(done - RIM, 0), arrived, done, ready, total)
        done = ready

    mean = jnp.sum(total, axis=1, keepdims=True)
    slope = jnp.sum(total * columns, axis=1, keepdims=True)
    lane = lax.broadcasted_iota(jnp.int32, (dates, 128), 1)
    mine[...] = jnp.where(lane == 0, mean, slope).T[0:8]
    start_all(sum_copy)
    slots[me] = mine[...]
    all_cols = lax.broadcasted_iota(jnp.int32, (1, cols), 1)
    all_cols = (2.0 * all_cols.astype(F32) + 1.0) / cols - 1.0
    square_sum = jnp.sum(all_cols * all_cols, axis=1, keepdims=True)
    finish_all(sum_copy)
    sums = lax.fori_loop(1, n, lambda s, acc: acc + slots[s], slots[0]).T
    date_mean = sums[:, 0:1] / (rows * cols)
    date_slope = sums[:, 1:2] / (rows * square_sum)
    trend[...] = date_mean + date_slope * columns

    def unplace(t, carry):
        gone = trend[pl.ds(t, 1), :]
        for q in range(rows // 8):
            piece = solved[pl.ds(q * 8 * dates + t, 8, stride=dates), :]
            series[t, q * 8 : q * 8 + 8, :] = piece - gone
        return carry

    lax.fori_loop(0, dates, unplace, 0, unroll=8)


def body(slc_tiles, look_weight, pair_list):
    n = lax.axis_size("gx")
    date_dev, _, rows, cols = slc_tiles.shape
    block = 16
    strip = cols // n
    dates = date_dev * n
    pitch = dates + 8
    halves = rows // block
    planned = (LAGS + 1) * dates
    chunks = 2 * halves
    most = block // 2 + RIM
    lines = 2 * halves * date_dev

    vmem = pl.BlockSpec(memory_space=pltpu.VMEM)
    anywhere = pl.BlockSpec(memory_space=pl.ANY)
    dma = pltpu.SemaphoreType.DMA
    return pl.pallas_call(
        functools.partial(kernel, n),
        out_shape=jax.ShapeDtypeStruct((dates, rows, strip), F32),
        in_specs=[anywhere, anywhere, vmem],
        out_specs=vmem,
        scratch_shapes=[
            pltpu.VMEM(slc_tiles.shape, BF16),
            pltpu.VMEM((chunks, date_dev, block, cols), BF16),
            pltpu.VMEM((chunks, dates, block, strip), BF16),
            pltpu.VMEM((n + 2, lines, 256), F32),
            pltpu.VMEM((n, lines, 128), BF16),
            pltpu.VMEM((n, lines, 128), BF16),
            pltpu.VMEM((3, rows, strip), F32),
            pltpu.VMEM((dates, LAGS * dates), F32),
            pltpu.VMEM((4, rows * pitch, strip), F32),
            pltpu.VMEM((4, halves * pitch, 128), F32),
            pltpu.VMEM((most, planned, strip), BF16),
            pltpu.VMEM((most, planned, strip), BF16),
            pltpu.VMEM((halves, planned, 128), BF16),
            pltpu.VMEM((halves, planned, 128), BF16),
            pltpu.VMEM((4, pitch, strip), F32),
            pltpu.VMEM((rows * dates, strip), F32),
            pltpu.VMEM((8, dates), F32),
            pltpu.VMEM((n, 8, dates), F32),
            pltpu.VMEM((dates, strip), F32),
            dma((chunks + 2, n)),
            dma((chunks + 2, n)),
            dma((4 + chunks,)),
        ],
        compiler_params=pltpu.CompilerParams(
            collective_id=0, has_side_effects=True, vmem_limit_bytes=60 * MIB
        ),
    )(slc_tiles, look_weight, pair_list.T)


def solution(mesh):
    return jax.shard_map(
        body,
        mesh=mesh,
        in_specs=(P("gx", None, "band", None), P("band", None), P()),
        out_specs=P(None, "band", "gx"),
        check_vma=False,
    )
```

```python
import functools
import math

import jax
import jax.numpy as jnp
from jax import lax
from jax.experimental import pallas as pl
from jax.experimental.pallas import tpu as pltpu
from jax.sharding import PartitionSpec as P

LOOK = 9
RIM = LOOK // 2
LAGS = 4
MESH = pl.DeviceIdType.MESH
F32 = jnp.float32
BF16 = jnp.bfloat16
HIGHEST = lax.Precision.HIGHEST
MIB = 1024 * 1024


def greet_all(n, band, me):
    barrier = pltpu.get_barrier_semaphore()

    def greet(k, carry):
        peer = lax.rem(me + k, n)
        pl.semaphore_signal(barrier, inc=1, device_id=(band, peer), device_id_type=MESH)
        return carry

    lax.fori_loop(1, n, greet, 0)
    pl.semaphore_wait(barrier, n - 1)


def split(values):
    high = values.astype(BF16)
    low = (values - high.astype(F32)).astype(BF16)
    return high, low


def dot_split(a, b):
    a_high, a_low = split(a)
    b_high, b_low = split(b)
    total = jnp.dot(a_high, b_high, preferred_element_type=F32)
    total = total + jnp.dot(a_high, b_low, preferred_element_type=F32)
    return total + jnp.dot(a_low, b_high, preferred_element_type=F32)


def network_weights(pairs, dates, degree_bound):
    pair_total = pairs.shape[1]
    first = pairs[0:1]
    second = pairs[1:2]
    ids = lax.broadcasted_iota(jnp.int32, (dates, pair_total), 0)
    incidence = (ids == first).astype(F32) - (ids == second).astype(F32)
    incidence_t = incidence.T
    product = jnp.dot(incidence.astype(BF16), incidence_t.astype(BF16), preferred_element_type=F32)
    row = lax.broadcasted_iota(jnp.int32, (dates, dates), 0)
    col = lax.broadcasted_iota(jnp.int32, (dates, dates), 1)
    eye = (row == col).astype(F32)
    normal = product + eye
    top = 1.0 + 2.0 * degree_bound
    scale = 2.0 / (1.0 + top)
    power = eye - normal * scale
    inverse = (eye + power) * scale
    terms = 2
    need = 18.5 * (top + 1.0) / 2.0
    while terms < need:
        power = dot_split(power, power)
        inverse = inverse + dot_split(inverse, power)
        terms *= 2
    rest = eye - jnp.dot(normal, inverse, precision=HIGHEST, preferred_element_type=F32)
    inverse = inverse + jnp.dot(inverse, rest, precision=HIGHEST, preferred_element_type=F32)
    combos = LAGS * dates
    key = (first + dates * (second - first - 1)).astype(F32)
    key = jnp.broadcast_to(key, (8, pair_total)).T[:, 0:1].astype(jnp.int32)
    combo = lax.broadcasted_iota(jnp.int32, (pair_total, combos), 1)
    count = jnp.sum((combo == key).astype(F32), axis=0, keepdims=True)
    combo = lax.broadcasted_iota(jnp.int32, (dates, combos), 1)
    lag = jnp.ones_like(combo)
    for step in range(1, LAGS):
        lag = lag + (combo >= step * dates).astype(jnp.int32)
    start = combo - dates * (lag - 1)
    date = lax.broadcasted_iota(jnp.int32, (dates, combos), 0)
    spread = ((date == start).astype(F32) - (date == start + lag).astype(F32)) * count
    return jnp.dot(inverse, spread, precision=HIGHEST, preferred_element_type=F32)


def cross(planes, first, second, rows):
    first = pl.ds(first, rows)
    second = pl.ds(second, rows)
    return planes[3, first, :] * planes[0, second, :] - planes[2, first, :] * planes[1, second, :]


def power(planes, first, rows):
    first = pl.ds(first, rows)
    return planes[2, first, :] * planes[0, first, :] + planes[3, first, :] * planes[1, first, :]


def window_sums(term, lo, hi, out_lo, out_hi):
    @functools.cache
    def ones(r):
        return term(r) if lo <= r < hi else None

    @functools.cache
    def run(r, size):
        if size == 1:
            return ones(r)
        a, b = run(r, size // 2), run(r + size // 2, size // 2)
        return b if a is None else a if b is None else a + b

    for r in range(out_lo, out_hi):
        total, last = run(r - RIM, LOOK - 1), ones(r + RIM)
        yield r, total if last is None else total + last


def kernel(
    n, slc, look_weight, pairs, series, trend,
    local, packed, images, rim_parts, rim_send, rim_recv, weight, weights, planes, rim_planes,
    high, low, rim_high, rim_low, powers, solved, mine, slots,
    send_sem, recv_sem, own_sem,
):
    band = lax.axis_index("band")
    me = lax.axis_index("gx")
    date_dev, _, rows, cols = slc.shape
    chunks, dates, block, strip = images.shape
    halves = chunks // 2
    part_rows = block // 2
    pitch = dates + 8
    groups = date_dev * 2 * halves

    def columns_of(j):
        return pl.ds(pl.multiple_of(j * strip, strip), strip)

    fetch = pltpu.make_async_copy(slc, local, own_sem.at[0])
    fetch.start()
    sides = (lax.max(me - 1, 0), me, lax.min(me + 1, n - 1))
    weight_copies = [
        pltpu.make_async_copy(look_weight.at[:, columns_of(j)], weight.at[i], own_sem.at[1 + i])
        for i, j in enumerate(sides)
    ]
    for copy in weight_copies:
        copy.start()
    own_tiles = [
        pltpu.make_async_copy(
            packed.at[c, :, :, columns_of(me)],
            images.at[c, pl.ds(me * date_dev, date_dev)],
            own_sem.at[4 + c],
        )
        for c in range(chunks)
    ]

    def pack(half):
        for d in range(date_dev):
            real = local[d, 0, half * block : half * block + block, :].astype(F32)
            imag = local[d, 1, half * block : half * block + block, :].astype(F32)
            for e in range(2):
                at = slice(e * part_rows, (e + 1) * part_rows)
                tile = jnp.concatenate([real[at], imag[at]], axis=0)
                packed[2 * half + e, d] = tile.astype(BF16)

    fetch.wait()
    pack(0)
    greet_all(n, band, me)

    def tile_copy(c, k, source):
        peer = lax.rem(me + k, n)
        return pltpu.make_async_remote_copy(
            src_ref=packed.at[c, :, :, columns_of(peer)],
            dst_ref=images.at[c, pl.ds(source * date_dev, date_dev)],
            send_sem=send_sem.at[c, k],
            recv_sem=recv_sem.at[c, k],
            device_id=(band, peer),
            device_id_type=MESH,
        )

    def rim_copy(k, source):
        peer = lax.rem(me + k, n)
        return pltpu.make_async_remote_copy(
            src_ref=rim_send.at[peer],
            dst_ref=rim_recv.at[source],
            send_sem=send_sem.at[chunks, k],
            recv_sem=recv_sem.at[chunks, k],
            device_id=(band, peer),
            device_id_type=MESH,
        )

    def sum_copy(k, source):
        return pltpu.make_async_remote_copy(
            src_ref=mine,
            dst_ref=slots.at[source],
            send_sem=send_sem.at[chunks + 1, k],
            recv_sem=recv_sem.at[chunks + 1, k],
            device_id=(band, lax.rem(me + k, n)),
            device_id_type=MESH,
        )

    def start_all(make):
        def start(k, carry):
            make(k, me).start()
            return carry

        lax.fori_loop(1, n, start, 0)

    def finish_all(make):
        def finish(k, carry):
            one = make(k, lax.rem(me + n - k, n))
            one.wait_send()
            one.wait_recv()
            return carry

        lax.fori_loop(1, n, finish, 0)

    start_all(functools.partial(tile_copy, 0))
    start_all(functools.partial(tile_copy, 1))

    a = lax.broadcasted_iota(jnp.int32, (strip, 256), 0)
    b = lax.broadcasted_iota(jnp.int32, (strip, 256), 1)
    h = b & 7
    pick = ((b < 128) & (h < RIM) & (a == strip - RIM + h)) | (
        (b >= 128) & (h >= RIM) & (a == h - RIM)
    )
    pick = jnp.where(pick, 1.0, 0.0)
    pick_half = pick.astype(BF16)
    tall = groups * block
    a = lax.broadcasted_iota(jnp.int32, (tall, 256), 0)
    b = lax.broadcasted_iota(jnp.int32, (tall, 256), 1)
    keep = jnp.where((a & (block - 1)) == ((b & 127) >> 3), 1.0, 0.0)
    a = lax.broadcasted_iota(jnp.int32, (groups, tall), 0)
    b = lax.broadcasted_iota(jnp.int32, (groups, tall), 1) >> 4
    gather = jnp.zeros((groups, tall), jnp.bool_)
    for d in range(date_dev):
        for ph in range(2 * halves):
            gather = gather | ((b == d * 2 * halves + ph) & (a == ph * date_dev + d))
    gather = jnp.where(gather, 1.0, 0.0).astype(BF16)
    empty = jnp.zeros((groups, 256), F32)
    rim_parts[0] = empty
    rim_parts[n + 1] = empty

    def pick_rims(j, carry):
        slab = local[:, :, :, columns_of(j)].reshape(tall, strip)
        spread = jnp.dot(slab, pick_half, preferred_element_type=F32) * keep
        rim_parts[j + 1] = jnp.dot(gather, spread.astype(BF16), preferred_element_type=F32)
        return carry

    lax.fori_loop(0, n, pick_rims, 0, unroll=4)

    def join_rims(j, carry):
        rim_send[j] = (rim_parts[j, :, 0:128] + rim_parts[j + 2, :, 128:256]).astype(BF16)
        return carry

    lax.fori_loop(0, n, join_rims, 0, unroll=4)
    start_all(rim_copy)
    for c in range(2, chunks):
        if c % 2 == 0:
            pack(c // 2)
        start_all(functools.partial(tile_copy, c))
    for copy in own_tiles:
        copy.start()
    rim_recv[me] = rim_send[me]

    weights[...] = network_weights(pairs[...], dates, 2.0 * (pairs.shape[1] // n))
    w_high, w_low = split(weights[...])
    mix = jnp.concatenate([w_high, w_low], axis=0)
    column_ids = me * strip + lax.broadcasted_iota(jnp.int32, (1, strip), 1)
    columns = (2.0 * column_ids.astype(F32) + 1.0) / cols - 1.0

    for copy in weight_copies:
        copy.wait()
    rim_weight = jnp.dot(
        weight[0], pick[:, 0:128], precision=HIGHEST, preferred_element_type=F32
    ) + jnp.dot(weight[2], pick[:, 128:256], precision=HIGHEST, preferred_element_type=F32)

    zero = jnp.zeros((8, strip), F32)
    for part in range(4):
        for r in range(rows):
            planes[part, r * pitch + dates : (r + 1) * pitch, :] = zero
        for half in range(halves):
            rim_planes[part, half * pitch + dates : (half + 1) * pitch, :] = zero
    for slot in range(powers.shape[0]):
        powers[slot, dates:pitch, :] = zero

    def place_chunk(chunk):
        row = chunk * part_rows

        def place(t, carry):
            tile = images[chunk, t].astype(F32)
            for part in range(2):
                plane = tile[part * part_rows : (part + 1) * part_rows]
                target = pl.ds(row * pitch + t, part_rows, stride=pitch)
                planes[part, target, :] = plane
                planes[part + 2, target, :] = plane * weight[1, row : row + part_rows, :]
            return carry

        lax.fori_loop(0, dates, place, 0, unroll=8)

    k = lax.broadcasted_iota(jnp.int32, (strip, strip), 0)
    c = lax.broadcasted_iota(jnp.int32, (strip, strip), 1)
    main = jnp.where(jnp.abs(k - c) <= RIM, 1.0, 0.0).astype(BF16)
    k = lax.broadcasted_iota(jnp.int32, (128, strip), 0)
    c = lax.broadcasted_iota(jnp.int32, (128, strip), 1)
    offset = k & 7
    rim_col = jnp.where(offset < RIM, offset - RIM, strip + offset - RIM)
    rim_near = jnp.where(jnp.abs(rim_col - c) <= RIM, 1.0, 0.0)
    together = powers.shape[0]

    def stage(lo, hi, out_lo, out_hi, total):
        def row_sums(b, carry):
            t0 = pl.multiple_of(b * block, block)
            for lag in range(LAGS + 1):
                where = pl.ds(pl.multiple_of(lag * dates + t0, block), block)

                def term(r):
                    first = r * pitch + t0
                    if lag == 0:
                        return power(planes, first, block)
                    return cross(planes, first, first + lag, block)

                for r, value in window_sums(term, lo, hi, out_lo, out_hi):
                    h, l = split(value)
                    high[r - out_lo, where, :] = h
                    low[r - out_lo, where, :] = l
            return carry

        lax.fori_loop(0, dates // block, row_sums, 0)

        def some_rows(g, total):
            looks = []
            for i in range(together):
                at = g * together + i
                r = at + out_lo
                half = lax.div(r, block)
                side = jnp.where((k >> 3) == lax.rem(r, block), rim_near, 0.0).astype(BF16)
                matrix = jnp.concatenate([main, side], axis=0)
                looked = jnp.dot(
                    jnp.concatenate([high[at], rim_high[half]], axis=1),
                    matrix,
                    preferred_element_type=F32,
                ) + jnp.dot(
                    jnp.concatenate([low[at], rim_low[half]], axis=1),
                    matrix,
                    preferred_element_type=F32,
                )
                powers[i, 0:dates, :] = looked[0:dates]
                looks.append(looked)
            sines = []
            for i in range(together):
                looked = looks[i]
                observed = []
                for lag in range(1, LAGS + 1):
                    both = looked[0:dates] * powers[i, lag : lag + dates, :]
                    sine = looked[lag * dates : (lag + 1) * dates] * lax.rsqrt(both + 1e-6)
                    observed.append(sine.astype(BF16))
                sines.append(jnp.concatenate(observed, axis=0))
            for i in range(0, together, 2):
                pair = jnp.concatenate(sines[i : i + 2], axis=1)
                both = jnp.dot(mix, pair, preferred_element_type=F32)
                value = both[0:dates] + both[dates:]
                for e in range(2):
                    r = g * together + i + e + out_lo
                    one = value[:, e * strip : (e + 1) * strip]
                    solved[pl.ds(pl.multiple_of(r * dates, dates), dates), :] = one
                    total = total + one
            return total

        return lax.fori_loop(0, (out_hi - out_lo) // together, some_rows, total)

    finish_all(functools.partial(tile_copy, 0))
    own_tiles[0].wait()
    place_chunk(0)
    finish_all(rim_copy)

    a = lax.broadcasted_iota(jnp.int32, (rows, 128), 0)
    b = lax.broadcasted_iota(jnp.int32, (rows, 128), 1)
    rim_weight = jnp.where((a & (block - 1)) == (b >> 3), rim_weight, 0.0)
    for half in range(halves):
        heavy = jnp.sum(rim_weight[half * block : half * block + block], axis=0, keepdims=True)
        for d in range(n):
            for part in range(2):
                at = (part * halves + half) * date_dev
                piece = rim_recv[d].astype(F32)[at : at + date_dev]
                target = half * pitch + d * date_dev
                rim_planes[part, target : target + date_dev, :] = piece
                rim_planes[part + 2, target : target + date_dev, :] = piece * heavy
    pieces = []
    for lag in range(LAGS + 1):
        line = []
        for half in range(halves):
            if lag == 0:
                line.append(power(rim_planes, half * pitch, dates))
            else:
                line.append(cross(rim_planes, half * pitch, half * pitch + lag, dates))
        pieces.append(jnp.concatenate(line, axis=1))
    lanes = rows * 8
    a = lax.broadcasted_iota(jnp.int32, (lanes, lanes), 0)
    b = lax.broadcasted_iota(jnp.int32, (lanes, lanes), 1)
    near = (jnp.abs((a >> 3) - (b >> 3)) <= RIM) & ((a & 7) == (b & 7))
    near = jnp.where(near, 1.0, 0.0).astype(BF16)
    h, l = split(jnp.concatenate(pieces, axis=0))
    rim_sum = jnp.dot(h, near, preferred_element_type=F32) + jnp.dot(
        l, near, preferred_element_type=F32
    )
    h, l = split(rim_sum)
    for half in range(halves):
        rim_high[half] = h[:, half * 128 : half * 128 + 128]
        rim_low[half] = l[:, half * 128 : half * 128 + 128]

    total = jnp.zeros((dates, strip), F32)
    done = 0
    for c in range(1, chunks):
        finish_all(functools.partial(tile_copy, c))
        own_tiles[c].wait()
        place_chunk(c)
        arrived = (c + 1) * part_rows
        ready = rows if c == chunks - 1 else arrived - RIM
        total = stage(max(done - RIM, 0), arrived, done, ready, total)
        done = ready

    mean = jnp.sum(total, axis=1, keepdims=True)
    slope = jnp.sum(total * columns, axis=1, keepdims=True)
    lane = lax.broadcasted_iota(jnp.int32, (dates, 128), 1)
    mine[...] = jnp.where(lane == 0, mean, slope).T[0:8]
    start_all(sum_copy)
    slots[me] = mine[...]

    def unplace(t, carry):
        for q in range(rows // 8):
            piece = solved[pl.ds(q * 8 * dates + t, 8, stride=dates), :]
            series[t, q * 8 : q * 8 + 8, :] = piece
        return carry

    lax.fori_loop(0, dates, unplace, 0, unroll=8)
    all_cols = lax.broadcasted_iota(jnp.int32, (1, cols), 1)
    all_cols = (2.0 * all_cols.astype(F32) + 1.0) / cols - 1.0
    square_sum = jnp.sum(all_cols * all_cols, axis=1, keepdims=True)
    finish_all(sum_copy)
    sums = lax.fori_loop(1, n, lambda s, acc: acc + slots[s], slots[0]).T
    date_mean = sums[:, 0:1] / (rows * cols)
    date_slope = sums[:, 1:2] / (rows * square_sum)
    trend[...] = date_mean + date_slope * columns


def remove_kernel(series, trend, corrected):
    for t in range(series.shape[0]):
        corrected[t] = series[t] - trend[t : t + 1, :]


def body(slc_tiles, look_weight, pair_list):
    n = lax.axis_size("gx")
    date_dev, _, rows, cols = slc_tiles.shape
    block = 16
    strip = cols // n
    dates = date_dev * n
    pitch = dates + 8
    halves = rows // block
    planned = (LAGS + 1) * dates
    chunks = 2 * halves
    most = block - RIM
    lines = 2 * halves * date_dev

    vmem = pl.BlockSpec(memory_space=pltpu.VMEM)
    anywhere = pl.BlockSpec(memory_space=pl.ANY)
    dma = pltpu.SemaphoreType.DMA
    series, trend = pl.pallas_call(
        functools.partial(kernel, n),
        out_shape=(
            jax.ShapeDtypeStruct((dates, rows, strip), F32),
            jax.ShapeDtypeStruct((dates, strip), F32),
        ),
        in_specs=[anywhere, anywhere, vmem],
        out_specs=(vmem, vmem),
        scratch_shapes=[
            pltpu.VMEM(slc_tiles.shape, BF16),
            pltpu.VMEM((chunks, date_dev, block, cols), BF16),
            pltpu.VMEM((chunks, dates, block, strip), BF16),
            pltpu.VMEM((n + 2, lines, 256), F32),
            pltpu.VMEM((n, lines, 128), BF16),
            pltpu.VMEM((n, lines, 128), BF16),
            pltpu.VMEM((3, rows, strip), F32),
            pltpu.VMEM((dates, LAGS * dates), F32),
            pltpu.VMEM((4, rows * pitch, strip), F32),
            pltpu.VMEM((4, halves * pitch, 128), F32),
            pltpu.VMEM((most, planned, strip), BF16),
            pltpu.VMEM((most, planned, strip), BF16),
            pltpu.VMEM((halves, planned, 128), BF16),
            pltpu.VMEM((halves, planned, 128), BF16),
            pltpu.VMEM((4, pitch, strip), F32),
            pltpu.VMEM((rows * dates, strip), F32),
            pltpu.VMEM((8, dates), F32),
            pltpu.VMEM((n, 8, dates), F32),
            dma((chunks + 2, n)),
            dma((chunks + 2, n)),
            dma((4 + chunks,)),
        ],
        compiler_params=pltpu.CompilerParams(
            collective_id=0, has_side_effects=True, vmem_limit_bytes=60 * MIB
        ),
    )(slc_tiles, look_weight, pair_list.T)

    part = min(dates, 16)
    cube = pl.BlockSpec((part, rows, strip), lambda i: (i, 0, 0))
    return pl.pallas_call(
        remove_kernel,
        grid=(dates // part,),
        out_shape=jax.ShapeDtypeStruct((dates, rows, strip), F32),
        in_specs=[cube, pl.BlockSpec((part, strip), lambda i: (i, 0))],
        out_specs=cube,
    )(series, trend)


def solution(mesh):
    return jax.shard_map(
        body,
        mesh=mesh,
        in_specs=(P("gx", None, "band", None), P("band", None), P()),
        out_specs=P(None, "band", "gx"),
        check_vma=False,
    )
```

```python
import functools
import math

import jax
import jax.numpy as jnp
from jax import lax
from jax.experimental import pallas as pl
from jax.experimental.pallas import tpu as pltpu
from jax.sharding import PartitionSpec as P

LOOK = 9
RIM = LOOK // 2
LAGS = 4
MESH = pl.DeviceIdType.MESH
F32 = jnp.float32
BF16 = jnp.bfloat16
HIGHEST = lax.Precision.HIGHEST
MIB = 1024 * 1024


def wrap(index, n):
    return jnp.where(index >= n, index - n, index)


def greet_all(n, band, me):
    barrier = pltpu.get_barrier_semaphore()

    def greet(k, carry):
        peer = wrap(me + k, n)
        pl.semaphore_signal(barrier, inc=1, device_id=(band, peer), device_id_type=MESH)
        return carry

    lax.fori_loop(1, n, greet, 0, unroll=True)
    pl.semaphore_wait(barrier, n - 1)


def split(values):
    high = values.astype(BF16)
    low = (values - high.astype(F32)).astype(BF16)
    return high, low


def dot_split(a, b):
    a_high, a_low = split(a)
    b_high, b_low = split(b)
    total = jnp.dot(a_high, b_high, preferred_element_type=F32)
    total = total + jnp.dot(a_high, b_low, preferred_element_type=F32)
    return total + jnp.dot(a_low, b_high, preferred_element_type=F32)


def network_weights(pairs, dates, degree_bound):
    pair_total = pairs.shape[1]
    first = pairs[0:1]
    second = pairs[1:2]
    ids = lax.broadcasted_iota(jnp.int32, (dates, pair_total), 0)
    incidence = (ids == first).astype(F32) - (ids == second).astype(F32)
    incidence_t = incidence.T
    product = jnp.dot(incidence.astype(BF16), incidence_t.astype(BF16), preferred_element_type=F32)
    row = lax.broadcasted_iota(jnp.int32, (dates, dates), 0)
    col = lax.broadcasted_iota(jnp.int32, (dates, dates), 1)
    eye = (row == col).astype(F32)
    normal = product + eye
    top = 1.0 + 2.0 * degree_bound
    scale = 2.0 / (1.0 + top)
    power = eye - normal * scale
    inverse = (eye + power) * scale
    terms = 2
    need = 18.5 * (top + 1.0) / 2.0
    while terms < need:
        power = dot_split(power, power)
        inverse = inverse + dot_split(inverse, power)
        terms *= 2
    rest = eye - jnp.dot(normal, inverse, precision=HIGHEST, preferred_element_type=F32)
    inverse = inverse + jnp.dot(inverse, rest, precision=HIGHEST, preferred_element_type=F32)
    combos = LAGS * dates
    key = (first + dates * (second - first - 1)).astype(F32)
    key = jnp.broadcast_to(key, (8, pair_total)).T[:, 0:1].astype(jnp.int32)
    combo = lax.broadcasted_iota(jnp.int32, (pair_total, combos), 1)
    count = jnp.sum((combo == key).astype(F32), axis=0, keepdims=True)
    combo = lax.broadcasted_iota(jnp.int32, (dates, combos), 1)
    lag = jnp.ones_like(combo)
    for step in range(1, LAGS):
        lag = lag + (combo >= step * dates).astype(jnp.int32)
    start = combo - dates * (lag - 1)
    date = lax.broadcasted_iota(jnp.int32, (dates, combos), 0)
    spread = ((date == start).astype(F32) - (date == start + lag).astype(F32)) * count
    return jnp.dot(inverse, spread, precision=HIGHEST, preferred_element_type=F32)


def cross(planes, first, second, rows):
    first = pl.ds(first, rows)
    second = pl.ds(second, rows)
    return planes[3, first, :] * planes[0, second, :] - planes[2, first, :] * planes[1, second, :]


def power(planes, first, rows):
    first = pl.ds(first, rows)
    return planes[2, first, :] * planes[0, first, :] + planes[3, first, :] * planes[1, first, :]


def window_sums(term, lo, hi, out_lo, out_hi):
    @functools.cache
    def ones(r):
        return term(r) if lo <= r < hi else None

    @functools.cache
    def run(r, size):
        if size == 1:
            return ones(r)
        a, b = run(r, size // 2), run(r + size // 2, size // 2)
        return b if a is None else a if b is None else a + b

    for r in range(out_lo, out_hi):
        total, last = run(r - RIM, LOOK - 1), ones(r + RIM)
        yield r, total if last is None else total + last


def kernel(
    n, slc, look_weight, pairs, series, trend,
    local, packed, images, rim_parts, rim_send, rim_recv, weight, weights, planes, rim_planes,
    high, low, rim_high, rim_low, powers, solved, mine, slots,
    send_sem, recv_sem, own_sem,
):
    band = lax.axis_index("band")
    me = lax.axis_index("gx")
    date_dev, _, rows, cols = slc.shape
    chunks, dates, block, strip = images.shape
    halves = chunks // 2
    part_rows = block // 2
    pitch = dates + 8
    groups = date_dev * 2 * halves

    def columns_of(j):
        return pl.ds(pl.multiple_of(j * strip, strip), strip)

    fetch = pltpu.make_async_copy(slc, local, own_sem.at[0])
    fetch.start()
    sides = (lax.max(me - 1, 0), me, lax.min(me + 1, n - 1))
    weight_copies = [
        pltpu.make_async_copy(look_weight.at[:, columns_of(j)], weight.at[i], own_sem.at[1 + i])
        for i, j in enumerate(sides)
    ]
    for copy in weight_copies:
        copy.start()
    def pack(half):
        for d in range(date_dev):
            real = local[d, 0, half * block : half * block + block, :].astype(F32)
            imag = local[d, 1, half * block : half * block + block, :].astype(F32)
            for e in range(2):
                at = slice(e * part_rows, (e + 1) * part_rows)
                tile = jnp.concatenate([real[at], imag[at]], axis=0)
                packed[2 * half + e, d] = tile.astype(BF16)

    fetch.wait()
    pack(0)
    greet_all(n, band, me)

    parts = [slice(0, 2)] + [slice(c, c + 1) for c in range(2, chunks)]
    rim_at, sum_at = len(parts), len(parts) + 1

    def tile_refs(part, peer):
        size = part.stop - part.start
        return (
            packed.at[pl.ds(part.start, size), :, :, columns_of(peer)],
            images.at[pl.ds(part.start, size), pl.ds(me * date_dev, date_dev)],
        )

    def rim_refs(peer):
        return rim_send.at[peer], rim_recv.at[me]

    def sum_refs(peer):
        return mine, slots.at[me]

    def start_all(at, refs_of):
        def start(k, carry):
            peer = wrap(me + k, n)
            source, target = refs_of(peer)
            pltpu.make_async_remote_copy(
                src_ref=source,
                dst_ref=target,
                send_sem=send_sem.at[at],
                recv_sem=recv_sem.at[at],
                device_id=(band, peer),
                device_id_type=MESH,
            ).start()
            return carry

        lax.fori_loop(1, n, start, 0, unroll=5)
        source, target = refs_of(me)
        pltpu.make_async_copy(source, target, recv_sem.at[at]).start()

    def start_tiles(at):
        start_all(at, functools.partial(tile_refs, parts[at]))

    def received(at, whole):
        pltpu.make_async_copy(whole, whole, recv_sem.at[at]).wait()

    def sent(at, others):
        pltpu.make_async_copy(others, others, send_sem.at[at]).wait()

    start_tiles(0)

    a = lax.broadcasted_iota(jnp.int32, (strip, 256), 0)
    b = lax.broadcasted_iota(jnp.int32, (strip, 256), 1)
    h = b & 7
    pick = ((b < 128) & (h < RIM) & (a == strip - RIM + h)) | (
        (b >= 128) & (h >= RIM) & (a == h - RIM)
    )
    pick = jnp.where(pick, 1.0, 0.0)
    pick_half = pick.astype(BF16)
    tall = groups * block
    a = lax.broadcasted_iota(jnp.int32, (tall, 256), 0)
    b = lax.broadcasted_iota(jnp.int32, (tall, 256), 1)
    keep = jnp.where((a & (block - 1)) == ((b & 127) >> 3), 1.0, 0.0)
    a = lax.broadcasted_iota(jnp.int32, (groups, tall), 0)
    b = lax.broadcasted_iota(jnp.int32, (groups, tall), 1) >> 4
    gather = jnp.zeros((groups, tall), jnp.bool_)
    for d in range(date_dev):
        for ph in range(2 * halves):
            gather = gather | ((b == d * 2 * halves + ph) & (a == ph * date_dev + d))
    gather = jnp.where(gather, 1.0, 0.0).astype(BF16)
    empty = jnp.zeros((groups, 256), F32)
    rim_parts[0] = empty
    rim_parts[n + 1] = empty

    def pick_rims(j, carry):
        slab = local[:, :, :, columns_of(j)].reshape(tall, strip)
        spread = jnp.dot(slab, pick_half, preferred_element_type=F32) * keep
        rim_parts[j + 1] = jnp.dot(gather, spread.astype(BF16), preferred_element_type=F32)
        return carry

    lax.fori_loop(0, n, pick_rims, 0, unroll=4)

    def join_rims(j, carry):
        rim_send[j] = (rim_parts[j, :, 0:128] + rim_parts[j + 2, :, 128:256]).astype(BF16)
        return carry

    lax.fori_loop(0, n, join_rims, 0, unroll=4)
    start_all(rim_at, rim_refs)
    for c in range(2, chunks):
        if c % 2 == 0:
            pack(c // 2)
        start_tiles(c - 1)

    weights[...] = network_weights(pairs[...], dates, 2.0 * (pairs.shape[1] // n))
    w_high, w_low = split(weights[...])
    mix = jnp.concatenate([w_high, w_low], axis=0)
    column_ids = me * strip + lax.broadcasted_iota(jnp.int32, (1, strip), 1)
    columns = (2.0 * column_ids.astype(F32) + 1.0) / cols - 1.0

    for copy in weight_copies:
        copy.wait()
    rim_weight = jnp.dot(
        weight[0], pick[:, 0:128], precision=HIGHEST, preferred_element_type=F32
    ) + jnp.dot(weight[2], pick[:, 128:256], precision=HIGHEST, preferred_element_type=F32)

    zero = jnp.zeros((8, strip), F32)
    for part in range(4):
        for r in range(rows):
            planes[part, r * pitch + dates : (r + 1) * pitch, :] = zero
        for half in range(halves):
            rim_planes[part, half * pitch + dates : (half + 1) * pitch, :] = zero
    for slot in range(powers.shape[0]):
        powers[slot, dates:pitch, :] = zero

    def place_chunk(chunk):
        row = chunk * part_rows

        def place(t, carry):
            tile = images[chunk, t].astype(F32)
            for part in range(2):
                plane = tile[part * part_rows : (part + 1) * part_rows]
                target = pl.ds(row * pitch + t, part_rows, stride=pitch)
                planes[part, target, :] = plane
                planes[part + 2, target, :] = plane * weight[1, row : row + part_rows, :]
            return carry

        lax.fori_loop(0, dates, place, 0, unroll=8)

    k = lax.broadcasted_iota(jnp.int32, (strip, strip), 0)
    c = lax.broadcasted_iota(jnp.int32, (strip, strip), 1)
    main = jnp.where(jnp.abs(k - c) <= RIM, 1.0, 0.0).astype(BF16)
    k = lax.broadcasted_iota(jnp.int32, (128, strip), 0)
    c = lax.broadcasted_iota(jnp.int32, (128, strip), 1)
    offset = k & 7
    rim_col = jnp.where(offset < RIM, offset - RIM, strip + offset - RIM)
    rim_near = jnp.where(jnp.abs(rim_col - c) <= RIM, 1.0, 0.0)
    together = powers.shape[0]

    def stage(lo, hi, out_lo, out_hi, total):
        def row_sums(b, carry):
            t0 = pl.multiple_of(b * block, block)
            for lag in range(LAGS + 1):
                where = pl.ds(pl.multiple_of(lag * dates + t0, block), block)

                def term(r):
                    first = r * pitch + t0
                    if lag == 0:
                        return power(planes, first, block)
                    return cross(planes, first, first + lag, block)

                for r, value in window_sums(term, lo, hi, out_lo, out_hi):
                    h, l = split(value)
                    high[r - out_lo, where, :] = h
                    low[r - out_lo, where, :] = l
            return carry

        lax.fori_loop(0, dates // block, row_sums, 0)

        def some_rows(g, total):
            looks = []
            for i in range(together):
                at = g * together + i
                r = at + out_lo
                half = lax.div(r, block)
                side = jnp.where((k >> 3) == lax.rem(r, block), rim_near, 0.0).astype(BF16)
                matrix = jnp.concatenate([main, side], axis=0)
                looked = jnp.dot(
                    jnp.concatenate([high[at], rim_high[half]], axis=1),
                    matrix,
                    preferred_element_type=F32,
                ) + jnp.dot(
                    jnp.concatenate([low[at], rim_low[half]], axis=1),
                    matrix,
                    preferred_element_type=F32,
                )
                powers[i, 0:dates, :] = looked[0:dates]
                looks.append(looked)
            sines = []
            for i in range(together):
                looked = looks[i]
                observed = []
                for lag in range(1, LAGS + 1):
                    both = looked[0:dates] * powers[i, lag : lag + dates, :]
                    sine = looked[lag * dates : (lag + 1) * dates] * lax.rsqrt(both + 1e-6)
                    observed.append(sine.astype(BF16))
                sines.append(jnp.concatenate(observed, axis=0))
            for i in range(0, together, 2):
                pair = jnp.concatenate(sines[i : i + 2], axis=1)
                both = jnp.dot(mix, pair, preferred_element_type=F32)
                value = both[0:dates] + both[dates:]
                for e in range(2):
                    r = g * together + i + e + out_lo
                    one = value[:, e * strip : (e + 1) * strip]
                    solved[pl.ds(pl.multiple_of(r * dates, dates), dates), :] = one
                    total = total + one
            return total

        return lax.fori_loop(0, (out_hi - out_lo) // together, some_rows, total)

    received(0, images.at[pl.ds(0, 2)])
    place_chunk(0)
    place_chunk(1)
    received(rim_at, rim_recv)

    a = lax.broadcasted_iota(jnp.int32, (rows, 128), 0)
    b = lax.broadcasted_iota(jnp.int32, (rows, 128), 1)
    rim_weight = jnp.where((a & (block - 1)) == (b >> 3), rim_weight, 0.0)
    for half in range(halves):
        heavy = jnp.sum(rim_weight[half * block : half * block + block], axis=0, keepdims=True)
        for d in range(n):
            for part in range(2):
                at = (part * halves + half) * date_dev
                piece = rim_recv[d].astype(F32)[at : at + date_dev]
                target = half * pitch + d * date_dev
                rim_planes[part, target : target + date_dev, :] = piece
                rim_planes[part + 2, target : target + date_dev, :] = piece * heavy
    pieces = []
    for lag in range(LAGS + 1):
        line = []
        for half in range(halves):
            if lag == 0:
                line.append(power(rim_planes, half * pitch, dates))
            else:
                line.append(cross(rim_planes, half * pitch, half * pitch + lag, dates))
        pieces.append(jnp.concatenate(line, axis=1))
    lanes = rows * 8
    a = lax.broadcasted_iota(jnp.int32, (lanes, lanes), 0)
    b = lax.broadcasted_iota(jnp.int32, (lanes, lanes), 1)
    near = (jnp.abs((a >> 3) - (b >> 3)) <= RIM) & ((a & 7) == (b & 7))
    near = jnp.where(near, 1.0, 0.0).astype(BF16)
    h, l = split(jnp.concatenate(pieces, axis=0))
    rim_sum = jnp.dot(h, near, preferred_element_type=F32) + jnp.dot(
        l, near, preferred_element_type=F32
    )
    h, l = split(rim_sum)
    for half in range(halves):
        rim_high[half] = h[:, half * 128 : half * 128 + 128]
        rim_low[half] = l[:, half * 128 : half * 128 + 128]

    total = jnp.zeros((dates, strip), F32)
    done = 0
    for c in range(1, chunks):
        if c > 1:
            received(c - 1, images.at[pl.ds(c, 1)])
            place_chunk(c)
        arrived = (c + 1) * part_rows
        ready = rows if c == chunks - 1 else arrived - RIM
        total = stage(max(done - RIM, 0), arrived, done, ready, total)
        done = ready

    mean = jnp.sum(total, axis=1, keepdims=True)
    slope = jnp.sum(total * columns, axis=1, keepdims=True)
    lane = lax.broadcasted_iota(jnp.int32, (dates, 128), 1)
    mine[...] = jnp.where(lane == 0, mean, slope).T[0:8]
    start_all(sum_at, sum_refs)

    def unplace(t, carry):
        for q in range(rows // 8):
            piece = solved[pl.ds(q * 8 * dates + t, 8, stride=dates), :]
            series[t, q * 8 : q * 8 + 8, :] = piece
        return carry

    lax.fori_loop(0, dates, unplace, 0, unroll=8)
    all_cols = lax.broadcasted_iota(jnp.int32, (1, cols), 1)
    all_cols = (2.0 * all_cols.astype(F32) + 1.0) / cols - 1.0
    square_sum = jnp.sum(all_cols * all_cols, axis=1, keepdims=True)
    received(sum_at, slots)
    others = pl.ds(0, (n - 1) * date_dev)
    for at, part in enumerate(parts):
        sent(at, images.at[pl.ds(part.start, part.stop - part.start), others])
    sent(rim_at, rim_recv.at[pl.ds(0, n - 1)])
    sent(sum_at, slots.at[pl.ds(0, n - 1)])
    sums = lax.fori_loop(1, n, lambda s, acc: acc + slots[s], slots[0]).T
    date_mean = sums[:, 0:1] / (rows * cols)
    date_slope = sums[:, 1:2] / (rows * square_sum)
    trend[...] = date_mean + date_slope * columns


def body(slc_tiles, look_weight, pair_list):
    n = lax.axis_size("gx")
    date_dev, _, rows, cols = slc_tiles.shape
    block = 16
    strip = cols // n
    dates = date_dev * n
    pitch = dates + 8
    halves = rows // block
    planned = (LAGS + 1) * dates
    chunks = 2 * halves
    most = block - RIM
    lines = 2 * halves * date_dev

    vmem = pl.BlockSpec(memory_space=pltpu.VMEM)
    anywhere = pl.BlockSpec(memory_space=pl.ANY)
    dma = pltpu.SemaphoreType.DMA
    series, trend = pl.pallas_call(
        functools.partial(kernel, n),
        out_shape=(
            jax.ShapeDtypeStruct((dates, rows, strip), F32),
            jax.ShapeDtypeStruct((dates, strip), F32),
        ),
        in_specs=[anywhere, anywhere, vmem],
        out_specs=(vmem, vmem),
        scratch_shapes=[
            pltpu.VMEM(slc_tiles.shape, BF16),
            pltpu.VMEM((chunks, date_dev, block, cols), BF16),
            pltpu.VMEM((chunks, dates, block, strip), BF16),
            pltpu.VMEM((n + 2, lines, 256), F32),
            pltpu.VMEM((n, lines, 128), BF16),
            pltpu.VMEM((n, lines, 128), BF16),
            pltpu.VMEM((3, rows, strip), F32),
            pltpu.VMEM((dates, LAGS * dates), F32),
            pltpu.VMEM((4, rows * pitch, strip), F32),
            pltpu.VMEM((4, halves * pitch, 128), F32),
            pltpu.VMEM((most, planned, strip), BF16),
            pltpu.VMEM((most, planned, strip), BF16),
            pltpu.VMEM((halves, planned, 128), BF16),
            pltpu.VMEM((halves, planned, 128), BF16),
            pltpu.VMEM((4, pitch, strip), F32),
            pltpu.VMEM((rows * dates, strip), F32),
            pltpu.VMEM((8, dates), F32),
            pltpu.VMEM((n, 8, dates), F32),
            dma((chunks + 1,)),
            dma((chunks + 1,)),
            dma((4,)),
        ],
        compiler_params=pltpu.CompilerParams(
            collective_id=0, has_side_effects=True, vmem_limit_bytes=60 * MIB
        ),
    )(slc_tiles, look_weight, pair_list.T)
    return series - trend[:, None, :]


def solution(mesh):
    return jax.shard_map(
        body,
        mesh=mesh,
        in_specs=(P("gx", None, "band", None), P("band", None), P()),
        out_specs=P(None, "band", "gx"),
        check_vma=False,
    )
```

```python
import functools
import math

import jax
import jax.numpy as jnp
from jax import lax
from jax.experimental import pallas as pl
from jax.experimental.pallas import tpu as pltpu
from jax.sharding import PartitionSpec as P

LOOK = 9
RIM = LOOK // 2
LAGS = 4
MESH = pl.DeviceIdType.MESH
F32 = jnp.float32
BF16 = jnp.bfloat16
HIGHEST = lax.Precision.HIGHEST
MIB = 1024 * 1024


def wrap(index, n):
    return jnp.where(index >= n, index - n, index)


def greet_all(n, band, me):
    barrier = pltpu.get_barrier_semaphore()

    def greet(k, carry):
        peer = wrap(me + k, n)
        pl.semaphore_signal(barrier, inc=1, device_id=(band, peer), device_id_type=MESH)
        return carry

    lax.fori_loop(1, n, greet, 0, unroll=True)
    return barrier


def split(values):
    high = values.astype(BF16)
    low = (values - high.astype(F32)).astype(BF16)
    return high, low


def dot_split(a, b):
    a_high, a_low = split(a)
    b_high, b_low = split(b)
    total = jnp.dot(a_high, b_high, preferred_element_type=F32)
    total = total + jnp.dot(a_high, b_low, preferred_element_type=F32)
    return total + jnp.dot(a_low, b_high, preferred_element_type=F32)


def network_weights(pairs, dates, degree_bound):
    pair_total = pairs.shape[1]
    first = pairs[0:1]
    second = pairs[1:2]
    ids = lax.broadcasted_iota(jnp.int32, (dates, pair_total), 0)
    incidence = (ids == first).astype(F32) - (ids == second).astype(F32)
    incidence_t = incidence.T
    product = jnp.dot(incidence.astype(BF16), incidence_t.astype(BF16), preferred_element_type=F32)
    row = lax.broadcasted_iota(jnp.int32, (dates, dates), 0)
    col = lax.broadcasted_iota(jnp.int32, (dates, dates), 1)
    eye = (row == col).astype(F32)
    normal = product + eye
    top = 1.0 + 2.0 * degree_bound
    scale = 2.0 / (1.0 + top)
    power = eye - normal * scale
    inverse = (eye + power) * scale
    terms = 2
    need = 18.5 * (top + 1.0) / 2.0
    while terms < need:
        power = dot_split(power, power)
        inverse = inverse + dot_split(inverse, power)
        terms *= 2
    rest = eye - jnp.dot(normal, inverse, precision=HIGHEST, preferred_element_type=F32)
    inverse = inverse + jnp.dot(inverse, rest, precision=HIGHEST, preferred_element_type=F32)
    combos = LAGS * dates
    key = (first + dates * (second - first - 1)).astype(F32)
    key = jnp.broadcast_to(key, (8, pair_total)).T[:, 0:1].astype(jnp.int32)
    combo = lax.broadcasted_iota(jnp.int32, (pair_total, combos), 1)
    count = jnp.sum((combo == key).astype(F32), axis=0, keepdims=True)
    combo = lax.broadcasted_iota(jnp.int32, (dates, combos), 1)
    lag = jnp.ones_like(combo)
    for step in range(1, LAGS):
        lag = lag + (combo >= step * dates).astype(jnp.int32)
    start = combo - dates * (lag - 1)
    date = lax.broadcasted_iota(jnp.int32, (dates, combos), 0)
    spread = ((date == start).astype(F32) - (date == start + lag).astype(F32)) * count
    return jnp.dot(inverse, spread, precision=HIGHEST, preferred_element_type=F32)


def cross(planes, first, second, rows):
    first = pl.ds(first, rows)
    second = pl.ds(second, rows)
    return planes[3, first, :] * planes[0, second, :] - planes[2, first, :] * planes[1, second, :]


def power(planes, first, rows):
    first = pl.ds(first, rows)
    return planes[2, first, :] * planes[0, first, :] + planes[3, first, :] * planes[1, first, :]


def window_sums(term, lo, hi, out_lo, out_hi):
    @functools.cache
    def ones(r):
        return term(r) if lo <= r < hi else None

    @functools.cache
    def run(r, size):
        if size == 1:
            return ones(r)
        a, b = run(r, size // 2), run(r + size // 2, size // 2)
        return b if a is None else a if b is None else a + b

    for r in range(out_lo, out_hi):
        total, last = run(r - RIM, LOOK - 1), ones(r + RIM)
        yield r, total if last is None else total + last


def kernel(
    n, slc, look_weight, pairs, series, trend,
    local, packed, images, rim_parts, rim_send, rim_recv, weight, weights, planes, rim_planes,
    high, low, rim_high, rim_low, powers, solved, mine, slots,
    send_sem, recv_sem, own_sem,
):
    band = lax.axis_index("band")
    me = lax.axis_index("gx")
    date_dev, _, rows, cols = slc.shape
    chunks, dates, block, strip = images.shape
    halves = chunks // 2
    part_rows = block // 2
    pitch = dates + 8
    groups = date_dev * 2 * halves

    def columns_of(j):
        return pl.ds(pl.multiple_of(j * strip, strip), strip)

    fetch = pltpu.make_async_copy(slc, local, own_sem.at[0])
    fetch.start()
    barrier = greet_all(n, band, me)
    sides = (lax.max(me - 1, 0), me, lax.min(me + 1, n - 1))
    weight_copies = [
        pltpu.make_async_copy(look_weight.at[:, columns_of(j)], weight.at[i], own_sem.at[1 + i])
        for i, j in enumerate(sides)
    ]
    for copy in weight_copies:
        copy.start()
    def pack(half):
        for d in range(date_dev):
            real = local[d, 0, half * block : half * block + block, :].astype(F32)
            imag = local[d, 1, half * block : half * block + block, :].astype(F32)
            for e in range(2):
                at = slice(e * part_rows, (e + 1) * part_rows)
                tile = jnp.concatenate([real[at], imag[at]], axis=0)
                packed[2 * half + e, d] = tile.astype(BF16)

    fetch.wait()
    pack(0)
    pl.semaphore_wait(barrier, n - 1)

    parts = [slice(0, 2)] + [slice(c, c + 1) for c in range(2, chunks)]
    rim_at, sum_at = len(parts), len(parts) + 1

    def tile_refs(part, peer):
        size = part.stop - part.start
        return (
            packed.at[pl.ds(part.start, size), :, :, columns_of(peer)],
            images.at[pl.ds(part.start, size), pl.ds(me * date_dev, date_dev)],
        )

    def rim_refs(peer):
        return rim_send.at[peer], rim_recv.at[me]

    def sum_refs(peer):
        return mine, slots.at[me]

    def start_all(at, refs_of):
        def start(i, carry):
            k = i + n // 2 - 1
            peer = wrap(me + jnp.where(k >= n, k - n + 1, k), n)
            source, target = refs_of(peer)
            pltpu.make_async_remote_copy(
                src_ref=source,
                dst_ref=target,
                send_sem=send_sem.at[at],
                recv_sem=recv_sem.at[at],
                device_id=(band, peer),
                device_id_type=MESH,
            ).start()
            return carry

        lax.fori_loop(1, n, start, 0, unroll=5)
        source, target = refs_of(me)
        pltpu.make_async_copy(source, target, recv_sem.at[at]).start()

    def start_tiles(at):
        start_all(at, functools.partial(tile_refs, parts[at]))

    def received(at, whole):
        pltpu.make_async_copy(whole, whole, recv_sem.at[at]).wait()

    def sent(at, others):
        pltpu.make_async_copy(others, others, send_sem.at[at]).wait()

    start_tiles(0)

    a = lax.broadcasted_iota(jnp.int32, (strip, 256), 0)
    b = lax.broadcasted_iota(jnp.int32, (strip, 256), 1)
    h = b & 7
    pick = ((b < 128) & (h < RIM) & (a == strip - RIM + h)) | (
        (b >= 128) & (h >= RIM) & (a == h - RIM)
    )
    pick = jnp.where(pick, 1.0, 0.0)
    pick_half = pick.astype(BF16)
    tall = groups * block
    a = lax.broadcasted_iota(jnp.int32, (tall, 256), 0)
    b = lax.broadcasted_iota(jnp.int32, (tall, 256), 1)
    keep = jnp.where((a & (block - 1)) == ((b & 127) >> 3), 1.0, 0.0)
    a = lax.broadcasted_iota(jnp.int32, (groups, tall), 0)
    b = lax.broadcasted_iota(jnp.int32, (groups, tall), 1) >> 4
    gather = jnp.zeros((groups, tall), jnp.bool_)
    for d in range(date_dev):
        for ph in range(2 * halves):
            gather = gather | ((b == d * 2 * halves + ph) & (a == ph * date_dev + d))
    gather = jnp.where(gather, 1.0, 0.0).astype(BF16)
    empty = jnp.zeros((groups, 256), F32)
    rim_parts[0] = empty
    rim_parts[n + 1] = empty

    def pick_rims(j, carry):
        slab = local[:, :, :, columns_of(j)].reshape(tall, strip)
        spread = jnp.dot(slab, pick_half, preferred_element_type=F32) * keep
        rim_parts[j + 1] = jnp.dot(gather, spread.astype(BF16), preferred_element_type=F32)
        return carry

    lax.fori_loop(0, n, pick_rims, 0, unroll=4)

    def join_rims(j, carry):
        rim_send[j] = (rim_parts[j, :, 0:128] + rim_parts[j + 2, :, 128:256]).astype(BF16)
        return carry

    lax.fori_loop(0, n, join_rims, 0, unroll=4)
    start_all(rim_at, rim_refs)
    for c in range(2, chunks):
        if c % 2 == 0:
            pack(c // 2)
        start_tiles(c - 1)

    weights[...] = network_weights(pairs[...], dates, 2.0 * (pairs.shape[1] // n))
    w_high, w_low = split(weights[...])
    mix = jnp.concatenate([w_high, w_low], axis=0)
    column_ids = me * strip + lax.broadcasted_iota(jnp.int32, (1, strip), 1)
    columns = (2.0 * column_ids.astype(F32) + 1.0) / cols - 1.0

    for copy in weight_copies:
        copy.wait()
    rim_weight = jnp.dot(
        weight[0], pick[:, 0:128], precision=HIGHEST, preferred_element_type=F32
    ) + jnp.dot(weight[2], pick[:, 128:256], precision=HIGHEST, preferred_element_type=F32)

    zero = jnp.zeros((8, strip), F32)
    for part in range(4):
        for r in range(rows):
            planes[part, r * pitch + dates : (r + 1) * pitch, :] = zero
        for half in range(halves):
            rim_planes[part, half * pitch + dates : (half + 1) * pitch, :] = zero
    for slot in range(powers.shape[0]):
        powers[slot, dates:pitch, :] = zero

    def place_chunk(chunk):
        row = chunk * part_rows

        def place(t, carry):
            tile = images[chunk, t].astype(F32)
            for part in range(2):
                plane = tile[part * part_rows : (part + 1) * part_rows]
                target = pl.ds(row * pitch + t, part_rows, stride=pitch)
                planes[part, target, :] = plane
                planes[part + 2, target, :] = plane * weight[1, row : row + part_rows, :]
            return carry

        lax.fori_loop(0, dates, place, 0, unroll=8)

    k = lax.broadcasted_iota(jnp.int32, (strip, strip), 0)
    c = lax.broadcasted_iota(jnp.int32, (strip, strip), 1)
    main = jnp.where(jnp.abs(k - c) <= RIM, 1.0, 0.0).astype(BF16)
    k = lax.broadcasted_iota(jnp.int32, (128, strip), 0)
    c = lax.broadcasted_iota(jnp.int32, (128, strip), 1)
    offset = k & 7
    rim_col = jnp.where(offset < RIM, offset - RIM, strip + offset - RIM)
    rim_near = jnp.where(jnp.abs(rim_col - c) <= RIM, 1.0, 0.0)
    together = powers.shape[0]

    def stage(lo, hi, out_lo, out_hi, total):
        def row_sums(b, carry):
            t0 = pl.multiple_of(b * block, block)
            for lag in range(LAGS + 1):
                where = pl.ds(pl.multiple_of(lag * dates + t0, block), block)

                def term(r):
                    first = r * pitch + t0
                    if lag == 0:
                        return power(planes, first, block)
                    return cross(planes, first, first + lag, block)

                for r, value in window_sums(term, lo, hi, out_lo, out_hi):
                    h, l = split(value)
                    high[r - out_lo, where, :] = h
                    low[r - out_lo, where, :] = l
            return carry

        lax.fori_loop(0, dates // block, row_sums, 0)

        def some_rows(g, total):
            looks = []
            for i in range(together):
                at = g * together + i
                r = at + out_lo
                half = lax.div(r, block)
                side = jnp.where((k >> 3) == lax.rem(r, block), rim_near, 0.0).astype(BF16)
                matrix = jnp.concatenate([main, side], axis=0)
                left = jnp.concatenate([high[at], low[at]], axis=0)
                right = jnp.concatenate([rim_high[half], rim_low[half]], axis=0)
                halved = jnp.dot(
                    jnp.concatenate([left, right], axis=1), matrix, preferred_element_type=F32
                )
                looked = halved[: (LAGS + 1) * dates] + halved[(LAGS + 1) * dates :]
                powers[i, 0:dates, :] = looked[0:dates]
                looks.append(looked)
            sines = []
            for i in range(together):
                looked = looks[i]
                observed = []
                for lag in range(1, LAGS + 1):
                    both = looked[0:dates] * powers[i, lag : lag + dates, :]
                    sine = looked[lag * dates : (lag + 1) * dates] * lax.rsqrt(both + 1e-6)
                    observed.append(sine.astype(BF16))
                sines.append(jnp.concatenate(observed, axis=0))
            for i in range(0, together, 2):
                pair = jnp.concatenate(sines[i : i + 2], axis=1)
                both = jnp.dot(mix, pair, preferred_element_type=F32)
                value = both[0:dates] + both[dates:]
                for e in range(2):
                    r = g * together + i + e + out_lo
                    one = value[:, e * strip : (e + 1) * strip]
                    solved[pl.ds(pl.multiple_of(r * dates, dates), dates), :] = one
                    total = total + one
            return total

        return lax.fori_loop(0, (out_hi - out_lo) // together, some_rows, total)

    received(0, images.at[pl.ds(0, 2)])
    place_chunk(0)
    place_chunk(1)
    received(rim_at, rim_recv)

    a = lax.broadcasted_iota(jnp.int32, (rows, 128), 0)
    b = lax.broadcasted_iota(jnp.int32, (rows, 128), 1)
    rim_weight = jnp.where((a & (block - 1)) == (b >> 3), rim_weight, 0.0)
    for half in range(halves):
        heavy = jnp.sum(rim_weight[half * block : half * block + block], axis=0, keepdims=True)
        for d in range(n):
            for part in range(2):
                at = (part * halves + half) * date_dev
                piece = rim_recv[d].astype(F32)[at : at + date_dev]
                target = half * pitch + d * date_dev
                rim_planes[part, target : target + date_dev, :] = piece
                rim_planes[part + 2, target : target + date_dev, :] = piece * heavy
    pieces = []
    for lag in range(LAGS + 1):
        line = []
        for half in range(halves):
            if lag == 0:
                line.append(power(rim_planes, half * pitch, dates))
            else:
                line.append(cross(rim_planes, half * pitch, half * pitch + lag, dates))
        pieces.append(jnp.concatenate(line, axis=1))
    lanes = rows * 8
    a = lax.broadcasted_iota(jnp.int32, (lanes, lanes), 0)
    b = lax.broadcasted_iota(jnp.int32, (lanes, lanes), 1)
    near = (jnp.abs((a >> 3) - (b >> 3)) <= RIM) & ((a & 7) == (b & 7))
    near = jnp.where(near, 1.0, 0.0).astype(BF16)
    h, l = split(jnp.concatenate(pieces, axis=0))
    rim_sum = jnp.dot(h, near, preferred_element_type=F32) + jnp.dot(
        l, near, preferred_element_type=F32
    )
    h, l = split(rim_sum)
    for half in range(halves):
        rim_high[half] = h[:, half * 128 : half * 128 + 128]
        rim_low[half] = l[:, half * 128 : half * 128 + 128]

    total = jnp.zeros((dates, strip), F32)
    done = 0
    for c in range(1, chunks):
        if c > 1:
            received(c - 1, images.at[pl.ds(c, 1)])
            place_chunk(c)
        arrived = (c + 1) * part_rows
        ready = rows if c == chunks - 1 else arrived - RIM
        total = stage(max(done - RIM, 0), arrived, done, ready, total)
        done = ready

    mean = jnp.sum(total, axis=1, keepdims=True)
    slope = jnp.sum(total * columns, axis=1, keepdims=True)
    lane = lax.broadcasted_iota(jnp.int32, (dates, 128), 1)
    mine[...] = jnp.where(lane == 0, mean, slope).T[0:8]
    start_all(sum_at, sum_refs)

    def unplace(t, carry):
        for q in range(rows // 8):
            piece = solved[pl.ds(q * 8 * dates + t, 8, stride=dates), :]
            series[t, q * 8 : q * 8 + 8, :] = piece
        return carry

    lax.fori_loop(0, dates, unplace, 0, unroll=8)
    all_cols = lax.broadcasted_iota(jnp.int32, (1, cols), 1)
    all_cols = (2.0 * all_cols.astype(F32) + 1.0) / cols - 1.0
    square_sum = jnp.sum(all_cols * all_cols, axis=1, keepdims=True)
    received(sum_at, slots)
    others = pl.ds(0, (n - 1) * date_dev)
    for at, part in enumerate(parts):
        sent(at, images.at[pl.ds(part.start, part.stop - part.start), others])
    sent(rim_at, rim_recv.at[pl.ds(0, n - 1)])
    sent(sum_at, slots.at[pl.ds(0, n - 1)])
    sums = lax.fori_loop(1, n, lambda s, acc: acc + slots[s], slots[0]).T
    date_mean = sums[:, 0:1] / (rows * cols)
    date_slope = sums[:, 1:2] / (rows * square_sum)
    trend[...] = date_mean + date_slope * columns


def body(slc_tiles, look_weight, pair_list):
    n = lax.axis_size("gx")
    date_dev, _, rows, cols = slc_tiles.shape
    block = 16
    strip = cols // n
    dates = date_dev * n
    pitch = dates + 8
    halves = rows // block
    planned = (LAGS + 1) * dates
    chunks = 2 * halves
    most = block - RIM
    lines = 2 * halves * date_dev

    vmem = pl.BlockSpec(memory_space=pltpu.VMEM)
    anywhere = pl.BlockSpec(memory_space=pl.ANY)
    dma = pltpu.SemaphoreType.DMA
    series, trend = pl.pallas_call(
        functools.partial(kernel, n),
        out_shape=(
            jax.ShapeDtypeStruct((dates, rows, strip), F32),
            jax.ShapeDtypeStruct((dates, strip), F32),
        ),
        in_specs=[anywhere, anywhere, vmem],
        out_specs=(vmem, vmem),
        scratch_shapes=[
            pltpu.VMEM(slc_tiles.shape, BF16),
            pltpu.VMEM((chunks, date_dev, block, cols), BF16),
            pltpu.VMEM((chunks, dates, block, strip), BF16),
            pltpu.VMEM((n + 2, lines, 256), F32),
            pltpu.VMEM((n, lines, 128), BF16),
            pltpu.VMEM((n, lines, 128), BF16),
            pltpu.VMEM((3, rows, strip), F32),
            pltpu.VMEM((dates, LAGS * dates), F32),
            pltpu.VMEM((4, rows * pitch, strip), F32),
            pltpu.VMEM((4, halves * pitch, 128), F32),
            pltpu.VMEM((most, planned, strip), BF16),
            pltpu.VMEM((most, planned, strip), BF16),
            pltpu.VMEM((halves, planned, 128), BF16),
            pltpu.VMEM((halves, planned, 128), BF16),
            pltpu.VMEM((4, pitch, strip), F32),
            pltpu.VMEM((rows * dates, strip), F32),
            pltpu.VMEM((8, dates), F32),
            pltpu.VMEM((n, 8, dates), F32),
            dma((chunks + 1,)),
            dma((chunks + 1,)),
            dma((4,)),
        ],
        compiler_params=pltpu.CompilerParams(
            collective_id=0, has_side_effects=True, vmem_limit_bytes=60 * MIB
        ),
    )(slc_tiles, look_weight, pair_list.T)
    return series - trend[:, None, :]


def solution(mesh):
    return jax.shard_map(
        body,
        mesh=mesh,
        in_specs=(P("gx", None, "band", None), P("band", None), P()),
        out_specs=P(None, "band", "gx"),
        check_vma=False,
    )
```

```python
import functools
import math

import jax
import jax.numpy as jnp
from jax import lax
from jax.experimental import pallas as pl
from jax.experimental.pallas import tpu as pltpu
from jax.sharding import PartitionSpec as P

LOOK = 9
RIM = LOOK // 2
LAGS = 4
MESH = pl.DeviceIdType.MESH
F32 = jnp.float32
BF16 = jnp.bfloat16
HIGHEST = lax.Precision.HIGHEST
MIB = 1024 * 1024


def wrap(index, n):
    return jnp.where(index >= n, index - n, index)


def greet_all(n, band, me):
    barrier = pltpu.get_barrier_semaphore()

    def greet(k, carry):
        peer = wrap(me + k, n)
        pl.semaphore_signal(barrier, inc=1, device_id=(band, peer), device_id_type=MESH)
        return carry

    lax.fori_loop(1, n, greet, 0, unroll=True)
    return barrier


def split(values):
    high = values.astype(BF16)
    low = (values - high.astype(F32)).astype(BF16)
    return high, low


def dot_split(a, b):
    a_high, a_low = split(a)
    b_high, b_low = split(b)
    total = jnp.dot(a_high, b_high, preferred_element_type=F32)
    total = total + jnp.dot(a_high, b_low, preferred_element_type=F32)
    return total + jnp.dot(a_low, b_high, preferred_element_type=F32)


def network_weights(pairs, dates, degree_bound):
    pair_total = pairs.shape[1]
    first = pairs[0:1]
    second = pairs[1:2]
    ids = lax.broadcasted_iota(jnp.int32, (dates, pair_total), 0)
    incidence = (ids == first).astype(F32) - (ids == second).astype(F32)
    incidence_t = incidence.T
    product = jnp.dot(incidence.astype(BF16), incidence_t.astype(BF16), preferred_element_type=F32)
    row = lax.broadcasted_iota(jnp.int32, (dates, dates), 0)
    col = lax.broadcasted_iota(jnp.int32, (dates, dates), 1)
    eye = (row == col).astype(F32)
    normal = product + eye
    top = 1.0 + 2.0 * degree_bound
    scale = 2.0 / (1.0 + top)
    power = eye - normal * scale
    inverse = (eye + power) * scale
    terms = 2
    need = 18.5 * (top + 1.0) / 2.0
    while terms < need:
        power = dot_split(power, power)
        inverse = inverse + dot_split(inverse, power)
        terms *= 2
    rest = eye - jnp.dot(normal, inverse, precision=HIGHEST, preferred_element_type=F32)
    inverse = inverse + jnp.dot(inverse, rest, precision=HIGHEST, preferred_element_type=F32)
    combos = LAGS * dates
    key = (first + dates * (second - first - 1)).astype(F32)
    key = jnp.broadcast_to(key, (8, pair_total)).T[:, 0:1].astype(jnp.int32)
    combo = lax.broadcasted_iota(jnp.int32, (pair_total, combos), 1)
    count = jnp.sum((combo == key).astype(F32), axis=0, keepdims=True)
    combo = lax.broadcasted_iota(jnp.int32, (dates, combos), 1)
    lag = jnp.ones_like(combo)
    for step in range(1, LAGS):
        lag = lag + (combo >= step * dates).astype(jnp.int32)
    start = combo - dates * (lag - 1)
    date = lax.broadcasted_iota(jnp.int32, (dates, combos), 0)
    spread = ((date == start).astype(F32) - (date == start + lag).astype(F32)) * count
    return jnp.dot(inverse, spread, precision=HIGHEST, preferred_element_type=F32)


def cross(planes, first, second, rows):
    first = pl.ds(first, rows)
    second = pl.ds(second, rows)
    return planes[3, first, :] * planes[0, second, :] - planes[2, first, :] * planes[1, second, :]


def power(planes, first, rows):
    first = pl.ds(first, rows)
    return planes[2, first, :] * planes[0, first, :] + planes[3, first, :] * planes[1, first, :]


def window_sums(term, lo, hi, out_lo, out_hi):
    @functools.cache
    def ones(r):
        return term(r) if lo <= r < hi else None

    @functools.cache
    def run(r, size):
        if size == 1:
            return ones(r)
        a, b = run(r, size // 2), run(r + size // 2, size // 2)
        return b if a is None else a if b is None else a + b

    for r in range(out_lo, out_hi):
        total, last = run(r - RIM, LOOK - 1), ones(r + RIM)
        yield r, total if last is None else total + last


def kernel(
    n, slc, look_weight, pairs, series, trend,
    local, packed, images, rim_parts, rim_send, rim_recv, weight, weights, planes, rim_planes,
    high, low, rim_high, rim_low, powers, solved, mine, slots,
    send_sem, recv_sem, own_sem,
):
    band = lax.axis_index("band")
    me = lax.axis_index("gx")
    date_dev, _, rows, cols = slc.shape
    chunks, dates, block, strip = images.shape
    halves = chunks // 2
    part_rows = block // 2
    pitch = dates + 8
    groups = date_dev * 2 * halves

    def columns_of(j):
        return pl.ds(pl.multiple_of(j * strip, strip), strip)

    fetch = pltpu.make_async_copy(slc, local, own_sem.at[0])
    fetch.start()
    barrier = greet_all(n, band, me)
    sides = (lax.max(me - 1, 0), me, lax.min(me + 1, n - 1))
    weight_copies = [
        pltpu.make_async_copy(look_weight.at[:, columns_of(j)], weight.at[i], own_sem.at[1 + i])
        for i, j in enumerate(sides)
    ]
    for copy in weight_copies:
        copy.start()
    def pack(half):
        for d in range(date_dev):
            real = local[d, 0, half * block : half * block + block, :].astype(F32)
            imag = local[d, 1, half * block : half * block + block, :].astype(F32)
            for e in range(2):
                at = slice(e * part_rows, (e + 1) * part_rows)
                tile = jnp.concatenate([real[at], imag[at]], axis=0)
                packed[2 * half + e, d] = tile.astype(BF16)

    fetch.wait()
    pack(0)
    pl.semaphore_wait(barrier, n - 1)

    parts = [slice(0, 2)] + [slice(c, c + 1) for c in range(2, chunks)]
    rim_at, sum_at = len(parts), len(parts) + 1

    def tile_refs(part, peer):
        size = part.stop - part.start
        return (
            packed.at[pl.ds(part.start, size), :, :, columns_of(peer)],
            images.at[pl.ds(part.start, size), pl.ds(me * date_dev, date_dev)],
        )

    def rim_refs(peer):
        return rim_send.at[peer], rim_recv.at[me]

    def sum_refs(peer):
        return mine, slots.at[me]

    def start_all(at, refs_of):
        def start(i, carry):
            k = i + n // 2 - 1
            peer = wrap(me + jnp.where(k >= n, k - n + 1, k), n)
            source, target = refs_of(peer)
            pltpu.make_async_remote_copy(
                src_ref=source,
                dst_ref=target,
                send_sem=send_sem.at[at],
                recv_sem=recv_sem.at[at],
                device_id=(band, peer),
                device_id_type=MESH,
            ).start()
            return carry

        lax.fori_loop(1, n, start, 0, unroll=5)
        source, target = refs_of(me)
        pltpu.make_async_copy(source, target, recv_sem.at[at]).start()

    def start_tiles(at):
        start_all(at, functools.partial(tile_refs, parts[at]))

    def received(at, whole):
        pltpu.make_async_copy(whole, whole, recv_sem.at[at]).wait()

    def sent(at, others):
        pltpu.make_async_copy(others, others, send_sem.at[at]).wait()

    start_tiles(0)

    a = lax.broadcasted_iota(jnp.int32, (strip, 256), 0)
    b = lax.broadcasted_iota(jnp.int32, (strip, 256), 1)
    h = b & 7
    pick = ((b < 128) & (h < RIM) & (a == strip - RIM + h)) | (
        (b >= 128) & (h >= RIM) & (a == h - RIM)
    )
    pick = jnp.where(pick, 1.0, 0.0)
    pick_half = pick.astype(BF16)
    tall = groups * block
    a = lax.broadcasted_iota(jnp.int32, (tall, 256), 0)
    b = lax.broadcasted_iota(jnp.int32, (tall, 256), 1)
    keep = jnp.where((a & (block - 1)) == ((b & 127) >> 3), 1.0, 0.0)
    a = lax.broadcasted_iota(jnp.int32, (groups, tall), 0)
    b = lax.broadcasted_iota(jnp.int32, (groups, tall), 1) >> 4
    gather = jnp.zeros((groups, tall), jnp.bool_)
    for d in range(date_dev):
        for ph in range(2 * halves):
            gather = gather | ((b == d * 2 * halves + ph) & (a == ph * date_dev + d))
    gather = jnp.where(gather, 1.0, 0.0).astype(BF16)
    empty = jnp.zeros((groups, 256), F32)
    rim_parts[0] = empty
    rim_parts[n + 1] = empty

    def pick_rims(j, carry):
        slab = local[:, :, :, columns_of(j)].reshape(tall, strip)
        spread = jnp.dot(slab, pick_half, preferred_element_type=F32) * keep
        rim_parts[j + 1] = jnp.dot(gather, spread.astype(BF16), preferred_element_type=F32)
        return carry

    lax.fori_loop(0, n, pick_rims, 0, unroll=4)

    def join_rims(j, carry):
        rim_send[j] = (rim_parts[j, :, 0:128] + rim_parts[j + 2, :, 128:256]).astype(BF16)
        return carry

    lax.fori_loop(0, n, join_rims, 0, unroll=4)
    start_all(rim_at, rim_refs)
    for c in range(2, chunks):
        if c % 2 == 0:
            pack(c // 2)
        start_tiles(c - 1)

    weights[...] = network_weights(pairs[...], dates, 2.0 * (pairs.shape[1] // n))
    w_high, w_low = split(weights[...])
    mix = jnp.concatenate([w_high, w_low], axis=0)
    column_ids = me * strip + lax.broadcasted_iota(jnp.int32, (1, strip), 1)
    columns = (2.0 * column_ids.astype(F32) + 1.0) / cols - 1.0

    for copy in weight_copies:
        copy.wait()
    rim_weight = jnp.dot(
        weight[0], pick[:, 0:128], precision=HIGHEST, preferred_element_type=F32
    ) + jnp.dot(weight[2], pick[:, 128:256], precision=HIGHEST, preferred_element_type=F32)

    zero = jnp.zeros((8, strip), F32)
    for part in range(4):
        for r in range(rows):
            planes[part, r * pitch + dates : (r + 1) * pitch, :] = zero
        for half in range(halves):
            rim_planes[part, half * pitch + dates : (half + 1) * pitch, :] = zero
    for slot in range(powers.shape[0]):
        powers[slot, dates:pitch, :] = zero

    def place_chunk(chunk):
        row = chunk * part_rows

        def place(t, carry):
            tile = images[chunk, t].astype(F32)
            for part in range(2):
                plane = tile[part * part_rows : (part + 1) * part_rows]
                target = pl.ds(row * pitch + t, part_rows, stride=pitch)
                planes[part, target, :] = plane
                planes[part + 2, target, :] = plane * weight[1, row : row + part_rows, :]
            return carry

        lax.fori_loop(0, dates, place, 0, unroll=16)

    k = lax.broadcasted_iota(jnp.int32, (strip, strip), 0)
    c = lax.broadcasted_iota(jnp.int32, (strip, strip), 1)
    main = jnp.where(jnp.abs(k - c) <= RIM, 1.0, 0.0).astype(BF16)
    k = lax.broadcasted_iota(jnp.int32, (128, strip), 0)
    c = lax.broadcasted_iota(jnp.int32, (128, strip), 1)
    offset = k & 7
    rim_col = jnp.where(offset < RIM, offset - RIM, strip + offset - RIM)
    rim_near = jnp.where(jnp.abs(rim_col - c) <= RIM, 1.0, 0.0)
    together = powers.shape[0]

    def stage(lo, hi, out_lo, out_hi, total):
        def row_sums(b, carry):
            t0 = pl.multiple_of(b * block, block)
            for lag in range(LAGS + 1):
                where = pl.ds(pl.multiple_of(lag * dates + t0, block), block)

                def term(r):
                    first = r * pitch + t0
                    if lag == 0:
                        return power(planes, first, block)
                    return cross(planes, first, first + lag, block)

                for r, value in window_sums(term, lo, hi, out_lo, out_hi):
                    h, l = split(value)
                    high[r - out_lo, where, :] = h
                    low[r - out_lo, where, :] = l
            return carry

        lax.fori_loop(0, dates // block, row_sums, 0)

        def some_rows(g, total):
            looks = []
            for i in range(together):
                at = g * together + i
                r = at + out_lo
                half = lax.div(r, block)
                side = jnp.where((k >> 3) == lax.rem(r, block), rim_near, 0.0).astype(BF16)
                matrix = jnp.concatenate([main, side], axis=0)
                left = jnp.concatenate([high[at], low[at]], axis=0)
                right = jnp.concatenate([rim_high[half], rim_low[half]], axis=0)
                halved = jnp.dot(
                    jnp.concatenate([left, right], axis=1), matrix, preferred_element_type=F32
                )
                looked = halved[: (LAGS + 1) * dates] + halved[(LAGS + 1) * dates :]
                powers[i, 0:dates, :] = looked[0:dates]
                looks.append(looked)
            sines = []
            for i in range(together):
                looked = looks[i]
                observed = []
                for lag in range(1, LAGS + 1):
                    both = looked[0:dates] * powers[i, lag : lag + dates, :]
                    sine = looked[lag * dates : (lag + 1) * dates] * lax.rsqrt(both + 1e-6)
                    observed.append(sine.astype(BF16))
                sines.append(jnp.concatenate(observed, axis=0))
            for i in range(0, together, 2):
                pair = jnp.concatenate(sines[i : i + 2], axis=1)
                both = jnp.dot(mix, pair, preferred_element_type=F32)
                value = both[0:dates] + both[dates:]
                for e in range(2):
                    r = g * together + i + e + out_lo
                    one = value[:, e * strip : (e + 1) * strip]
                    solved[pl.ds(pl.multiple_of(r * dates, dates), dates), :] = one
                    total = total + one
            return total

        return lax.fori_loop(0, (out_hi - out_lo) // together, some_rows, total)

    received(0, images.at[pl.ds(0, 2)])
    place_chunk(0)
    place_chunk(1)
    received(rim_at, rim_recv)

    a = lax.broadcasted_iota(jnp.int32, (rows, 128), 0)
    b = lax.broadcasted_iota(jnp.int32, (rows, 128), 1)
    rim_weight = jnp.where((a & (block - 1)) == (b >> 3), rim_weight, 0.0)
    for half in range(halves):
        heavy = jnp.sum(rim_weight[half * block : half * block + block], axis=0, keepdims=True)
        for d in range(n):
            for part in range(2):
                at = (part * halves + half) * date_dev
                piece = rim_recv[d].astype(F32)[at : at + date_dev]
                target = half * pitch + d * date_dev
                rim_planes[part, target : target + date_dev, :] = piece
                rim_planes[part + 2, target : target + date_dev, :] = piece * heavy
    pieces = []
    for lag in range(LAGS + 1):
        line = []
        for half in range(halves):
            if lag == 0:
                line.append(power(rim_planes, half * pitch, dates))
            else:
                line.append(cross(rim_planes, half * pitch, half * pitch + lag, dates))
        pieces.append(jnp.concatenate(line, axis=1))
    lanes = rows * 8
    a = lax.broadcasted_iota(jnp.int32, (lanes, lanes), 0)
    b = lax.broadcasted_iota(jnp.int32, (lanes, lanes), 1)
    near = (jnp.abs((a >> 3) - (b >> 3)) <= RIM) & ((a & 7) == (b & 7))
    near = jnp.where(near, 1.0, 0.0).astype(BF16)
    h, l = split(jnp.concatenate(pieces, axis=0))
    rim_sum = jnp.dot(h, near, preferred_element_type=F32) + jnp.dot(
        l, near, preferred_element_type=F32
    )
    h, l = split(rim_sum)
    for half in range(halves):
        rim_high[half] = h[:, half * 128 : half * 128 + 128]
        rim_low[half] = l[:, half * 128 : half * 128 + 128]

    total = jnp.zeros((dates, strip), F32)
    done = 0
    for c in range(1, chunks):
        if c > 1:
            received(c - 1, images.at[pl.ds(c, 1)])
            place_chunk(c)
        arrived = (c + 1) * part_rows
        ready = rows if c == chunks - 1 else arrived - RIM
        total = stage(max(done - RIM, 0), arrived, done, ready, total)
        done = ready

    mean = jnp.sum(total, axis=1, keepdims=True)
    slope = jnp.sum(total * columns, axis=1, keepdims=True)
    lane = lax.broadcasted_iota(jnp.int32, (dates, 128), 1)
    mine[...] = jnp.where(lane == 0, mean, slope).T[0:8]
    start_all(sum_at, sum_refs)

    def unplace(t, carry):
        for q in range(rows // 8):
            piece = solved[pl.ds(q * 8 * dates + t, 8, stride=dates), :]
            series[t, q * 8 : q * 8 + 8, :] = piece
        return carry

    lax.fori_loop(0, dates, unplace, 0, unroll=8)
    all_cols = lax.broadcasted_iota(jnp.int32, (1, cols), 1)
    all_cols = (2.0 * all_cols.astype(F32) + 1.0) / cols - 1.0
    square_sum = jnp.sum(all_cols * all_cols, axis=1, keepdims=True)
    received(sum_at, slots)
    sums = lax.fori_loop(1, n, lambda s, acc: acc + slots[s], slots[0], unroll=True).T
    date_mean = sums[:, 0:1] / (rows * cols)
    date_slope = sums[:, 1:2] / (rows * square_sum)
    trend[...] = date_mean + date_slope * columns
    others = pl.ds(0, (n - 1) * date_dev)
    for at, part in enumerate(parts):
        sent(at, images.at[pl.ds(part.start, part.stop - part.start), others])
    sent(rim_at, rim_recv.at[pl.ds(0, n - 1)])
    sent(sum_at, slots.at[pl.ds(0, n - 1)])


def body(slc_tiles, look_weight, pair_list):
    n = lax.axis_size("gx")
    date_dev, _, rows, cols = slc_tiles.shape
    block = 16
    strip = cols // n
    dates = date_dev * n
    pitch = dates + 8
    halves = rows // block
    planned = (LAGS + 1) * dates
    chunks = 2 * halves
    most = block - RIM
    lines = 2 * halves * date_dev

    vmem = pl.BlockSpec(memory_space=pltpu.VMEM)
    anywhere = pl.BlockSpec(memory_space=pl.ANY)
    dma = pltpu.SemaphoreType.DMA
    series, trend = pl.pallas_call(
        functools.partial(kernel, n),
        out_shape=(
            jax.ShapeDtypeStruct((dates, rows, strip), F32),
            jax.ShapeDtypeStruct((dates, strip), F32),
        ),
        in_specs=[anywhere, anywhere, vmem],
        out_specs=(vmem, vmem),
        scratch_shapes=[
            pltpu.VMEM(slc_tiles.shape, BF16),
            pltpu.VMEM((chunks, date_dev, block, cols), BF16),
            pltpu.VMEM((chunks, dates, block, strip), BF16),
            pltpu.VMEM((n + 2, lines, 256), F32),
            pltpu.VMEM((n, lines, 128), BF16),
            pltpu.VMEM((n, lines, 128), BF16),
            pltpu.VMEM((3, rows, strip), F32),
            pltpu.VMEM((dates, LAGS * dates), F32),
            pltpu.VMEM((4, (rows + 1) * pitch, strip), F32),
            pltpu.VMEM((4, halves * pitch, 128), F32),
            pltpu.VMEM((most, planned, strip), BF16),
            pltpu.VMEM((most, planned, strip), BF16),
            pltpu.VMEM((halves, planned, 128), BF16),
            pltpu.VMEM((halves, planned, 128), BF16),
            pltpu.VMEM((4, pitch, strip), F32),
            pltpu.VMEM(((rows + 1) * dates, strip), F32),
            pltpu.VMEM((8, dates), F32),
            pltpu.VMEM((n, 8, dates), F32),
            dma((chunks + 1,)),
            dma((chunks + 1,)),
            dma((4,)),
        ],
        compiler_params=pltpu.CompilerParams(
            collective_id=0, has_side_effects=True, vmem_limit_bytes=60 * MIB
        ),
    )(slc_tiles, look_weight, pair_list.T)
    return series - trend[:, None, :]


def solution(mesh):
    return jax.shard_map(
        body,
        mesh=mesh,
        in_specs=(P("gx", None, "band", None), P("band", None), P()),
        out_specs=P(None, "band", "gx"),
        check_vma=False,
    )
```
